32 devices in a mesh: ctx: 8 (over z, y), head: 4 (over x, core).
Axes of the slice: x: 2, y: 2, z: 4, core: 2. Of those that a mesh axis runs over, the one named last changes fastest.
Arguments:
- conv_input: bfloat16 [6144, 8448], P(('ctx', 'head')), may hold values from -6 to 6
- conv_weight: float32 [4, 8448], replicated, may hold values from -3 to 3
- conv_bias: float32 [8448], replicated, may hold values from -3 to 3
- step_size: float32 [128, 6144], P('head', 'ctx'), may hold values from 0 to 0.12, as said below
- log_decay: float32 [128, 6144], P('head', 'ctx'), may hold values from -0.6 to 0, as said below
- skip_gain: float32 [128], P('head'), may hold values from 0.5 to 2
- grad_output: bfloat16 [6144, 8192], P('ctx', 'head'), may hold values from -6 to 6
Outputs:
- layer_output: bfloat16 [6144, 8192], P('ctx', 'head')
- grad_input: bfloat16 [6144, 8448], P(('ctx', 'head'))
- grad_step: float32 [128, 6144], P('head', 'ctx')
- grad_decay: float32 [128, 6144], P('head', 'ctx')
The draws below stay inside these ranges and needn't reach their ends.
Inputs may be any that keep to these rules, and one draw needn't show every extreme that they name: `step_size`: positive step sizes. `log_decay`: negative logarithms of decays.
All inputs are finite; a program needn't handle non-finite values.
Results may differ from the reference program's by a relative error of at most 0.013.
Values may be sent and summed in bfloat16 or wider, within the bound.
A program may use at most 128 MiB of HBM per device.

```python
import math
from functools import partial
import jax
import jax.numpy as jnp
from jax import lax

HEADS = 128
HEAD_DIM = 64
STATE = 128
CONV_W = 4
BLOCK = 256
INNER = 8192
CONV_CH = 8448
SEQ_DEV = 768
SEQ = 6144
N_HEAD = 4


def rate_fields(key):
    keys = jax.random.split(jax.random.fold_in(key, 7), 8)
    pick = jax.random.uniform(keys[0], (HEADS, 1))
    fast_share = 0.5
    quick_mode = pick < fast_share
    fast_rate = jnp.exp(jax.random.uniform(keys[1], (HEADS, 1), minval=math.log(1.0 / 50.0), maxval=math.log(1.0 / 30.0)))
    slow_rate = jnp.exp(jax.random.uniform(keys[2], (HEADS, 1), minval=math.log(0.05), maxval=math.log(0.5))) / SEQ
    baseline_rate = jnp.where(quick_mode, fast_rate, slow_rate)
    coarse_estimate = jax.random.uniform(keys[3], (HEADS, SEQ), minval=0.5, maxval=1.5)
    split_factor = jnp.exp(jax.random.uniform(keys[4], (HEADS, SEQ // SEQ_DEV), minval=math.log(0.5), maxval=math.log(1.5)))
    split_factor = jnp.repeat(split_factor, SEQ_DEV, axis=1)
    spots = jax.random.randint(keys[5], (2,), 0, SEQ)
    positions = jnp.arange(SEQ)
    match_tally = ((positions == spots[0]) | (positions == spots[1])).astype(jnp.float32)[None, :]
    loss_values = jax.random.uniform(keys[6], (HEADS, 1), minval=0.2, maxval=0.4)
    spike_events = jnp.where(quick_mode, 0.0, jnp.log(1.0 - loss_values)) * match_tally
    decay_factors = -baseline_rate * coarse_estimate * split_factor + spike_events
    steps_drawn = 0.4 * jnp.sqrt(baseline_rate) * jax.random.uniform(keys[7], (HEADS, SEQ), minval=0.5, maxval=1.5)
    return (steps_drawn.astype(jnp.float32), decay_factors.astype(jnp.float32))


def draw_step_size(key, part):
    return rate_fields(key)[0]


def draw_log_decay(key, part):
    return rate_fields(key)[1]


def block_scale(rng, dims, pieces, smallest, top_value):
    level = 1.0
    for dim, parts in pieces:
        steps = jax.random.uniform(jax.random.fold_in(jax.random.fold_in(rng, 6), dim), (parts,), jnp.float32, smallest / len(pieces), top_value / len(pieces))
        level = level * jnp.repeat(jnp.exp(steps), dims[dim] // parts).reshape((-1,) + (1,) * (len(dims) - 1 - dim))
    return level


def centred(key, shape, width, most, shards=(), dtype=jnp.bfloat16):
    level = block_scale(key, shape, shards, -0.22, 0.18) if shards else 1.0
    values = jax.random.normal(key, shape, jnp.float32) * width * level
    return jnp.minimum(jnp.maximum(values, -most), most).astype(dtype)


def setup_inputs(seed: int = 0) -> dict:
    splits = jax.random.split(jax.random.key(seed), 8)
    conv_input = centred(splits[0], (SEQ, CONV_CH), 1.0, 6.0, ((0, 32),))
    conv_weight = centred(splits[1], (CONV_W, CONV_CH), CONV_W ** -0.5, 3.0, (), jnp.float32)
    conv_bias = centred(splits[2], (CONV_CH,), 0.5, 3.0, (), jnp.float32)
    step_size = draw_step_size(jax.random.fold_in(splits[7], 71), 0)
    log_decay = draw_log_decay(jax.random.fold_in(splits[7], 71), 0)
    skip_gain = jnp.clip(0.5 + 1.5 * jax.random.uniform(splits[5], (HEADS,), jnp.float32) ** block_scale(splits[5], (HEADS,), ((0, 4),), -0.2, 0.2), 0.5, 2.0)
    grad_output = centred(splits[6], (SEQ, INNER), 1.0, 6.0, ((0, 8), (1, 4)))
    return dict(conv_input=conv_input, conv_weight=conv_weight, conv_bias=conv_bias, step_size=step_size, log_decay=log_decay, skip_gain=skip_gain, grad_output=grad_output)


def block_increment(features, step_sizes, input_map, log_rates):
    cumulative = jnp.cumsum(log_rates, axis=1)
    to_end = jnp.exp(cumulative[:, -1:] - cumulative) * step_sizes
    weighted = (input_map[None, :, :] * to_end[:, :, None]).astype(jnp.bfloat16)
    increment = jnp.einsum('hsn,shp->hnp', weighted.astype(jnp.float32), features.astype(jnp.float32))
    return (cumulative, increment)

def block_update(skip_gain, carry_state, inputs):
    features, step_sizes, input_map, output_map, log_rates = inputs
    cumulative, increment = block_increment(features, step_sizes, input_map, log_rates)
    length = log_rates.shape[1]
    row_index = lax.broadcasted_iota(jnp.int32, (length, length), 0)
    col_index = lax.broadcasted_iota(jnp.int32, (length, length), 1)
    causal = (row_index >= col_index)[None]
    log_gap = jnp.where(causal, cumulative[:, :, None] - cumulative[:, None, :], 0.0)
    decay_matrix = jnp.where(causal, jnp.exp(log_gap), 0.0)
    affinity = jnp.dot(output_map.astype(jnp.bfloat16), input_map.astype(jnp.bfloat16).T, preferred_element_type=jnp.float32)
    weights = (affinity[None] * decay_matrix * step_sizes[:, None, :]).astype(jnp.bfloat16)
    inside = jnp.einsum('hts,shp->thp', weights.astype(jnp.float32), features.astype(jnp.float32))
    entry_map = (output_map[None, :, :] * jnp.exp(cumulative)[:, :, None]).astype(jnp.bfloat16)
    carried = jnp.einsum('htn,hnp->thp', entry_map.astype(jnp.float32), carry_state.astype(jnp.bfloat16).astype(jnp.float32))
    output = inside + carried + skip_gain[None, :, None] * features.astype(jnp.float32)
    following = jnp.exp(cumulative[:, -1])[:, None, None] * carry_state + increment
    return (following, output)

def sequence_ssd(features, step_sizes, input_map, output_map, log_rates, skip_gain, entering):
    heads_here = step_sizes.shape[0]
    seq_rows = features.shape[0]
    blocks = seq_rows // BLOCK
    head_dim = features.shape[1] // heads_here
    feats_b = features.reshape(blocks, BLOCK, heads_here, head_dim)
    steps_b = step_sizes.reshape(heads_here, blocks, BLOCK).transpose(1, 0, 2)
    input_b = input_map.reshape(blocks, BLOCK, input_map.shape[1])
    output_b = output_map.reshape(blocks, BLOCK, output_map.shape[1])
    rates_b = log_rates.reshape(heads_here, blocks, BLOCK).transpose(1, 0, 2)
    update = jax.checkpoint(partial(block_update, skip_gain))
    leaving, outputs = lax.scan(update, entering, (feats_b, steps_b, input_b, output_b, rates_b))
    return (outputs.reshape(seq_rows, features.shape[1]), leaving)

def conv_forward(conv_input, conv_weight, conv_bias):
    taps_count = conv_weight.shape[0]
    tok_rows = conv_input.shape[0]
    padded = jnp.concatenate([jnp.zeros((taps_count - 1, conv_input.shape[1]), jnp.float32), conv_input.astype(jnp.float32)], axis=0)
    preact = conv_bias[None, :] + conv_weight[0][None, :] * padded[0:tok_rows]
    for offset in range(1, taps_count):
        preact = preact + conv_weight[offset][None, :] * padded[offset:offset + tok_rows]
    return preact

def reference(conv_input, conv_weight, conv_bias, step_size, log_decay, skip_gain, grad_output):
    group_heads = HEADS // N_HEAD

    def forward(inputs_conv, steps_all, rates_all):
        preact = conv_forward(inputs_conv, conv_weight, conv_bias)
        activated = jax.nn.silu(preact).astype(jnp.bfloat16)
        features = activated[:, :INNER].reshape(SEQ, N_HEAD, group_heads * HEAD_DIM).transpose(1, 0, 2)
        input_map = activated[:, INNER:INNER + STATE].astype(jnp.float32)
        output_map = activated[:, INNER + STATE:].astype(jnp.float32)
        input_groups = jnp.broadcast_to(input_map[None], (N_HEAD, SEQ, STATE))
        output_groups = jnp.broadcast_to(output_map[None], (N_HEAD, SEQ, STATE))
        steps_groups = steps_all.reshape(N_HEAD, group_heads, SEQ)
        rates_groups = rates_all.reshape(N_HEAD, group_heads, SEQ)
        skip_groups = skip_gain.reshape(N_HEAD, group_heads)
        entering = jnp.zeros((N_HEAD, group_heads, STATE, HEAD_DIM), jnp.float32)
        outputs, leaving = jax.vmap(sequence_ssd)(features, steps_groups, input_groups, output_groups, rates_groups, skip_groups, entering)
        return outputs.transpose(1, 0, 2).reshape(SEQ, INNER)
    output_full, pullback = jax.vjp(forward, conv_input, step_size, log_decay)
    grad_input, grad_step, grad_decay = pullback(grad_output.astype(jnp.float32))
    return (output_full.astype(jnp.bfloat16), grad_input, grad_step, grad_decay)
```

```python
from functools import partial

import jax
import jax.numpy as jnp
from jax import lax
from jax.experimental import pallas as pl
from jax.experimental.pallas import tpu as pltpu
from jax.sharding import PartitionSpec as P

STATE = 128
BLOCK = 256
GROUP = 8
TILE = 128
F32 = jnp.float32
BF16 = jnp.bfloat16
VMEM_LIMIT = 60 * 1024 * 1024
MESH = pl.DeviceIdType.MESH


def dot(a, b, ca, cb):
    return lax.dot_general(
        a, b, (((ca,), (cb,)), ((), ())), preferred_element_type=F32
    )


def head_of_lane(rows, width, head_dim):
    row = lax.broadcasted_iota(jnp.int32, (rows, width), 0)
    lane = lax.broadcasted_iota(jnp.int32, (rows, width), 1)
    return jnp.where(lax.rem(row, GROUP) == lane // head_dim, 1.0, 0.0).astype(BF16)


def expand(rows, width, head_dim):
    high = rows.astype(BF16).astype(F32)
    both = jnp.concatenate([high, rows - high], axis=0).astype(BF16)
    return dot(both, head_of_lane(2 * GROUP, width, head_dim), 0, 0)


def head_sums(value, head_dim):
    pick = head_of_lane(2 * GROUP, value.shape[1], head_dim)
    high = value.astype(BF16)
    low = (value - high.astype(F32)).astype(BF16)
    return (dot(pick, high, 1, 1) + dot(pick, low, 1, 1))[:GROUP]


def triangular(rows, contract):
    length = rows.shape[1]
    row = lax.broadcasted_iota(jnp.int32, (length, length), 0)
    col = lax.broadcasted_iota(jnp.int32, (length, length), 1)
    upper = jnp.where(row <= col, 1.0, 0.0).astype(BF16)
    high = rows.astype(BF16).astype(F32)
    rest = rows - high
    middle = rest.astype(BF16).astype(F32)
    terms = jnp.concatenate([high, middle, rest - middle, jnp.zeros_like(rows)], axis=0)
    sums = dot(terms.astype(BF16), upper, 1, contract)
    return sums[:GROUP] + sums[GROUP : 2 * GROUP] + sums[2 * GROUP : 3 * GROUP]


def at(start, size):
    return pl.ds(pl.multiple_of(start, size), size)


def mixer_kernel(
    H, C, head_dim,
    cin, cw, cb, step, rate, skip, dy,
    y, gin, gs, gd,
    halo, act, actm, dsil, xbuf, mbuf, cums, aff, da, inc, gp, dec,
    t_ref, r_ref, d_ref, tsend, inbox, outbox, ent, s_ref, g_ref, dots,
    gs1, gc1, dxbuf, rbuf, acc, gms, gmr, hsend, hrecv,
    halo_sem, x_send, x_recv, m_send, m_recv, t_send, t_recv, e_send, e_recv,
    b_send, b_recv, g_send, g_recv, h_send, h_recv,
):
    taps = cw.shape[0]
    TR, channels = cin.shape
    SR, lanes = dy.shape
    K, _, W = xbuf.shape
    NB = SR // BLOCK
    TPC = W // TILE
    inner = H * lanes
    c = lax.axis_index("ctx")
    head = lax.axis_index("head")
    index = c * H + head
    total = C * H
    order = sorted(range(1, H), key=lambda o: abs(o - H // 2))

    def where_is(i):
        return (i // H, i % H)

    following = where_is((index + 1) % total)
    preceding = where_is((index + total - 1) % total)

    barrier = pltpu.get_barrier_semaphore()
    for o in range(1, H):
        pl.semaphore_signal(barrier, inc=1, device_id=(c, (head + o) % H), device_id_type=MESH)
    for o in range(1, C):
        pl.semaphore_signal(barrier, inc=1, device_id=((c + o) % C, head), device_id_type=MESH)
    for who in (following, preceding):
        pl.semaphore_signal(barrier, inc=1, device_id=who, device_id_type=MESH)
    pl.semaphore_wait(barrier, H + C)

    def remote(src, dst, send, recv, who):
        return pltpu.make_async_remote_copy(
            src_ref=src, dst_ref=dst, send_sem=send, recv_sem=recv, device_id=who, device_id_type=MESH
        )

    halo_copy = remote(cin.at[pl.ds(TR - 16, 16)], halo, halo_sem.at[0], halo_sem.at[1], following)

    @pl.when(index < total - 1)
    def _():
        halo_copy.start()

    @pl.when(index > 0)
    def _():
        halo_copy.wait_recv()

    @pl.when(index == 0)
    def _():
        halo[...] = jnp.zeros_like(halo)

    def convolve(col):
        where = at(col, TILE)
        body = cin[:, where].astype(F32)
        padded = jnp.concatenate([halo[:, where].astype(F32)[8:], body], axis=0)
        first = 8 - (taps - 1)
        pre = cb[:, where] + cw[0:1, where] * padded[first : first + TR]
        for tap in range(1, taps):
            pre = pre + cw[tap : tap + 1, where] * padded[first + tap : first + tap + TR]
        sig = 0.5 * jnp.tanh(0.5 * pre) + 0.5
        value = pre * sig
        dsil[:, where] = (sig + value * (1.0 - sig)).astype(BF16)
        return value.astype(BF16)

    def peer(o):
        return (head + o) % H

    def source(o):
        return (head + H - o) % H

    def send_maps(o):
        return remote(actm, mbuf.at[at(head * TR, TR)], m_send.at[o], m_recv.at[o], (c, peer(o)))

    def recv_maps(o):
        return remote(actm, mbuf.at[at(source(o) * TR, TR)], m_send.at[o], m_recv.at[o], (c, peer(o)))

    def send_x(k, o):
        return remote(
            act.at[k, peer(o)], xbuf.at[k, at(head * TR, TR)], x_send.at[k, o], x_recv.at[k, o], (c, peer(o))
        )

    def recv_x(k, o):
        return remote(
            act.at[k, peer(o)], xbuf.at[k, at(source(o) * TR, TR)], x_send.at[k, o], x_recv.at[k, o], (c, peer(o))
        )

    for i in range(2 * STATE // TILE):
        actm[:, i * TILE : (i + 1) * TILE] = convolve(inner + i * TILE)
    for o in order:
        send_maps(o).start()
    mbuf[at(head * TR, TR), :] = actm[...]

    def conv_chunk(k, carry):
        for o in order + [0]:
            p = peer(o)
            for i in range(TPC):
                value = convolve(p * lanes + k * W + i * TILE)
                if o:
                    act[k, p, :, i * TILE : (i + 1) * TILE] = value
                else:
                    xbuf[k, at(head * TR, TR), i * TILE : (i + 1) * TILE] = value
            if o:
                send_x(k, o).start()
        return carry

    lax.fori_loop(0, K, conv_chunk, 0)

    def sums_chunk(k, carry):
        for b in range(NB):
            cums[k, b] = triangular(rate[at(k * GROUP, GROUP), b * BLOCK : (b + 1) * BLOCK], 0)
        return carry

    lax.fori_loop(0, K, sums_chunk, 0)

    for o in order:
        recv_maps(o).wait_recv()

    row = lax.broadcasted_iota(jnp.int32, (BLOCK, BLOCK), 0)
    col = lax.broadcasted_iota(jnp.int32, (BLOCK, BLOCK), 1)
    causal = row >= col
    for b in range(NB):
        m = mbuf[b * BLOCK : (b + 1) * BLOCK]
        aff[b] = jnp.where(causal, dot(m[:, STATE:], m[:, :STATE], 1, 1), 0.0)
        da[b] = jnp.zeros((BLOCK, BLOCK), F32)
    acc[...] = jnp.zeros_like(acc)

    def owner(k, j):
        return (k * TPC + j) % C

    def send_tile(k, j):
        return remote(tsend.at[k, j], inbox.at[k, c], t_send.at[k, j], t_recv.at[k, c], (owner(k, j), head))

    def recv_tile(k, src):
        return remote(tsend.at[k, 0], inbox.at[k, src], t_send.at[k, 0], t_recv.at[k, src], (src, head))

    def states(k):
        t_ref[...] = jnp.zeros_like(t_ref)
        r_ref[...] = jnp.zeros_like(r_ref)
        d_ref[...] = jnp.ones_like(d_ref)

        def block(b, carry):
            rows = at(b * BLOCK, BLOCK)
            x = xbuf[k, rows, :]
            cum = cums[k, b]
            last = cum[:, BLOCK - 1 :]
            to_end = expand(jnp.exp(last - cum) * step[at(k * GROUP, GROUP), rows], W, head_dim)
            from_start = expand(jnp.exp(cum), W, head_dim)
            xw = (x.astype(F32) * to_end).astype(BF16)
            dyw = (dy[rows, at(k * W, W)].astype(F32) * from_start).astype(BF16)
            more = dot(mbuf[rows, :STATE], xw, 0, 0)
            grad = dot(mbuf[rows, STATE:], dyw, 0, 0)
            last_dec = from_start[BLOCK - 1 :]
            inc[k, b] = more
            gp[k, b] = grad
            dec[k, b] = jnp.broadcast_to(last_dec, (GROUP, W))
            t_ref[...] = t_ref[...] * last_dec + more
            r_ref[...] = r_ref[...] + d_ref[0:1] * grad
            d_ref[...] = d_ref[...] * last_dec
            return carry

        lax.fori_loop(0, NB, block, 0)
        decay = d_ref[...]
        high = decay.astype(BF16).astype(F32)
        both = jnp.concatenate([high, decay - high], axis=0).astype(BF16)
        for j in range(TPC):
            where = slice(j * TILE, (j + 1) * TILE)
            tsend[k, j, :STATE] = t_ref[:, where].astype(BF16)
            tsend[k, j, STATE : 2 * STATE] = r_ref[:, where].astype(BF16)
            tsend[k, j, 2 * STATE :] = both[:, where]

        for j in range(TPC):
            @pl.when(owner(k, j) == c)
            def _():
                inbox[k, c] = tsend[k, j]

            @pl.when(owner(k, j) != c)
            def _():
                send_tile(k, j).start()

    def send_enter(k, j, dst):
        return remote(outbox.at[k, dst], ent.at[k, j], e_send.at[k, dst], e_recv.at[k, j], (dst, head))

    def chain(k):
        j = (c + total * TPC - k * TPC) % C

        @pl.when(j < TPC)
        def _():
            def arrive(src, carry):
                @pl.when(src != c)
                def _():
                    recv_tile(k, src).wait_recv()
                return carry

            lax.fori_loop(0, C, arrive, 0)

            def decay(src):
                both = inbox[k, src, 2 * STATE :].astype(F32)
                return both[0:1] + both[GROUP : GROUP + 1]

            def ahead(i, state):
                outbox[k, i, :STATE] = state.astype(BF16)
                return decay(i) * state + inbox[k, i, :STATE].astype(F32)

            def astern(i, grad):
                i = C - 1 - i
                outbox[k, i, STATE:] = grad.astype(BF16)
                return decay(i) * grad + inbox[k, i, STATE : 2 * STATE].astype(F32)

            lax.fori_loop(0, C, ahead, jnp.zeros((STATE, TILE), F32))
            lax.fori_loop(0, C, astern, jnp.zeros((STATE, TILE), F32))

            def leave(dst, carry):
                @pl.when(dst != c)
                def _():
                    send_enter(k, j, dst).start()
                return carry

            lax.fori_loop(0, C, leave, 0)
            ent[k, j] = outbox[k, c]

    def intra(k):
        pair = 2 * head_dim
        lane = lax.broadcasted_iota(jnp.int32, (BLOCK, pair), 1)

        def block(b, carry):
            rows = at(b * BLOCK, BLOCK)
            heads = at(k * GROUP, GROUP)
            wide = at(k * W, W)
            cum = cums[k, b]
            cum_col = cum.T
            x = xbuf[k, rows, :].astype(F32)
            dyb = dy[rows, wide]
            steps = expand(step[heads, rows], W, head_dim)
            xs = (x * steps).astype(BF16)
            ins_parts, back_parts = [], []
            for p in range(GROUP // 2):
                part = slice(p * pair, (p + 1) * pair)
                xs_p, dy_p = xs[:, part], dyb[:, part]
                ins, back = 0.0, 0.0
                for side in range(2):
                    h = 2 * p + side
                    mine = (lane // head_dim) == side
                    xs_h = jnp.where(mine, xs_p, jnp.zeros_like(xs_p))
                    dy_h = jnp.where(mine, dy_p, jnp.zeros_like(dy_p))
                    decay = jnp.exp(jnp.minimum(cum_col[:, h : h + 1] - cum[h : h + 1, :], 0.0))
                    weights = (aff[b] * decay).astype(BF16)
                    ins = ins + dot(weights, xs_h, 1, 0)
                    back = back + dot(weights, dy_h, 0, 0)
                    da[b] += dot(dy_h, xs_p, 1, 1) * decay
                ins_parts.append(ins)
                back_parts.append(back)
            ins = jnp.concatenate(ins_parts, axis=1)
            back = jnp.concatenate(back_parts, axis=1)
            gain = skip[0:1, wide]
            dyf = dyb.astype(F32)
            y[rows, wide] = (ins + gain * x).astype(BF16)
            dxbuf[k, rows, :] = (steps * back + gain * dyf).astype(BF16)
            gs1[k, b] = head_sums(x * back, head_dim)
            gc1[k, b] = head_sums(dyf * ins - xs.astype(F32) * back, head_dim)
            return carry

        lax.fori_loop(0, NB, block, 0)

    def send_back(k, o):
        return remote(
            dxbuf.at[k, at(peer(o) * TR, TR)], rbuf.at[k, head], b_send.at[k, o], b_recv.at[k, o], (c, peer(o))
        )

    def recv_back(k, o):
        return remote(
            dxbuf.at[k, at(peer(o) * TR, TR)], rbuf.at[k, source(o)], b_send.at[k, o], b_recv.at[k, o], (c, peer(o))
        )

    def carry_over(k):
        for j in range(TPC):
            @pl.when(owner(k, j) != c)
            def _():
                remote(
                    outbox.at[k, 0], ent.at[k, j], e_send.at[k, 0], e_recv.at[k, j], (owner(k, j), head)
                ).wait_recv()

        state = jnp.concatenate([ent[k, j, :STATE] for j in range(TPC)], axis=1).astype(F32)
        grad = jnp.concatenate([ent[k, j, STATE:] for j in range(TPC)], axis=1).astype(F32)
        grads = [None] * NB
        for b in range(NB - 1, -1, -1):
            grads[b] = grad
            g_ref[b] = grad.astype(BF16)
            if b > 0:
                grad = dec[k, b, 0:1] * grad + gp[k, b]
        for b in range(NB):
            s_ref[b] = state.astype(BF16)
            state = dec[k, b, 0:1] * state + inc[k, b]
            both = jnp.sum(state * grads[b], axis=0, keepdims=True)
            dots[b] = head_sums(jnp.broadcast_to(both, (TILE, W)), head_dim)

        def block(b, carry):
            rows = at(b * BLOCK, BLOCK)
            heads = at(k * GROUP, GROUP)
            wide = at(k * W, W)
            cum = cums[k, b]
            ending = jnp.exp(cum[:, BLOCK - 1 :] - cum)
            weight = ending * step[heads, rows]
            from_start = expand(jnp.exp(cum), W, head_dim)
            to_end = expand(weight, W, head_dim)
            x = xbuf[k, rows, :].astype(F32)
            dyf = dy[rows, wide].astype(F32)
            enter, leave = s_ref[b], g_ref[b]
            in_map, out_map = mbuf[rows, :STATE], mbuf[rows, STATE:]
            carried = from_start * dot(out_map, enter, 1, 0)
            pulled = dot(in_map, leave, 1, 0)
            y[rows, wide] = (y[rows, wide].astype(F32) + carried).astype(BF16)
            dxbuf[k, rows, :] = (dxbuf[k, rows, :].astype(F32) + to_end * pulled).astype(BF16)
            xq = head_sums(x * pulled, head_dim)
            gs[heads, rows] = gs1[k, b] + ending * xq
            gc = gc1[k, b] + head_sums(dyf * carried, head_dim) - weight * xq
            place = lax.broadcasted_iota(jnp.int32, gc.shape, 1)
            gc = gc + jnp.where(place == BLOCK - 1, dots[b][:, 0:1], 0.0)
            gd[heads, rows] = triangular(gc, 1)
            acc[rows, :STATE] += dot((x * to_end).astype(BF16), leave, 1, 1)
            acc[rows, STATE:] += dot((dyf * from_start).astype(BF16), enter, 1, 1)
            return carry

        lax.fori_loop(0, NB, block, 0)
        for o in order:
            send_back(k, o).start()
        rbuf[k, head] = dxbuf[k, at(head * TR, TR), :]

    def stage(k, carry):
        @pl.when(k < K)
        def _():
            for o in order:
                recv_x(k, o).wait_recv()
            states(k)

        @pl.when((k >= 1) & (k <= K))
        def _():
            chain(k - 1)

        @pl.when(k >= 2)
        def _():
            carry_over(k - 2)

        @pl.when(k < K)
        def _():
            intra(k)

        return carry

    lax.fori_loop(0, K + 2, stage, 0)

    def send_mapgrad(o):
        return remote(gms.at[at(peer(o) * TR, TR)], gmr.at[head], g_send.at[o], g_recv.at[o], (c, peer(o)))

    def recv_mapgrad(o):
        return remote(gms.at[at(peer(o) * TR, TR)], gmr.at[source(o)], g_send.at[o], g_recv.at[o], (c, peer(o)))

    for b in range(NB):
        rows = slice(b * BLOCK, (b + 1) * BLOCK)
        grad = jnp.where(causal, da[b], 0.0).astype(BF16)
        gms[rows, :STATE] = (acc[rows, :STATE] + dot(grad, mbuf[rows, STATE:], 0, 0)).astype(BF16)
        gms[rows, STATE:] = (acc[rows, STATE:] + dot(grad, mbuf[rows, :STATE], 1, 0)).astype(BF16)
    for o in order:
        send_mapgrad(o).start()
    gmr[head] = gms[at(head * TR, TR), :]

    def send_edge(k, wide):
        return remote(
            hsend.at[k, :, pl.ds(0, wide)], hrecv.at[k, :, pl.ds(0, wide)], h_send.at[k], h_recv.at[k], preceding
        )

    def edge(k, wide):
        @pl.when(index > 0)
        def _():
            send_edge(k, wide).start()

    def arrive_edge(k, wide):
        @pl.when(index < total - 1)
        def _():
            send_edge(k, wide).wait_recv()

        @pl.when(index == total - 1)
        def _():
            hrecv[k] = jnp.zeros(hrecv.shape[1:], F32)

    def unwind(grad_pre, tail, where):
        padded = jnp.concatenate([grad_pre, tail], axis=0)
        out = cw[taps - 1 : taps, where] * grad_pre
        for tap in range(taps - 2, -1, -1):
            begin = taps - 1 - tap
            out = out + cw[tap : tap + 1, where] * padded[begin : begin + TR]
        gin[:, where] = out.astype(BF16)

    def first_rows(k):
        for o in order:
            recv_back(k, o).wait_recv()
        for p in range(H):
            where = at(p * lanes + k * W, W)
            top = rbuf[k, p, :16].astype(F32) * dsil[:16, where].astype(F32)
            hsend[k, :, p * W : (p + 1) * W] = top[:8]
        edge(k, H * W)

    def last_rows(k):
        arrive_edge(k, H * W)
        for p in range(H):
            for i in range(TPC):
                where = at(p * lanes + k * W + i * TILE, TILE)
                inside = slice(i * TILE, (i + 1) * TILE)
                grad_pre = rbuf[k, p, :, inside].astype(F32) * dsil[:, where].astype(F32)
                unwind(grad_pre, hrecv[k, :, p * W + i * TILE : p * W + (i + 1) * TILE], where)

    def final(k, carry):
        @pl.when(k < K)
        def _():
            first_rows(k)

        @pl.when(k >= 1)
        def _():
            last_rows(k - 1)

        return carry

    lax.fori_loop(0, K + 1, final, 0)

    for o in order:
        recv_mapgrad(o).wait_recv()
    parts = []
    for i in range(2 * STATE // TILE):
        inside = slice(i * TILE, (i + 1) * TILE)
        summed = gmr[0, :, inside].astype(F32)
        for p in range(1, H):
            summed = summed + gmr[p, :, inside].astype(F32)
        grad_pre = summed.astype(BF16).astype(F32) * dsil[:, inner + i * TILE : inner + (i + 1) * TILE].astype(F32)
        parts.append(grad_pre)
        hsend[K, :, inside] = grad_pre[:8]
    edge(K, 2 * STATE)
    arrive_edge(K, 2 * STATE)
    for i in range(2 * STATE // TILE):
        inside = slice(i * TILE, (i + 1) * TILE)
        unwind(parts[i], hrecv[K, :, inside], slice(inner + i * TILE, inner + (i + 1) * TILE))

    @pl.when(index < total - 1)
    def _():
        halo_copy.wait_send()

    for o in order:
        send_maps(o).wait_send()
        send_mapgrad(o).wait_send()

    def drain(k, carry):
        for o in order:
            send_x(k, o).wait_send()
            send_back(k, o).wait_send()
        for j in range(TPC):
            @pl.when(owner(k, j) != c)
            def _():
                send_tile(k, j).wait_send()
        mine = (c + total * TPC - k * TPC) % C

        @pl.when(mine < TPC)
        def _():
            def leave(dst, carry):
                @pl.when(dst != c)
                def _():
                    send_enter(k, mine, dst).wait_send()
                return carry

            lax.fori_loop(0, C, leave, 0)

        return carry

    lax.fori_loop(0, K, drain, 0)

    @pl.when(index > 0)
    def _():
        def drain_edges(k, carry):
            send_edge(k, H * W).wait_send()
            return carry

        lax.fori_loop(0, K, drain_edges, 0)
        send_edge(K, 2 * STATE).wait_send()


def local(conv_input, conv_weight, conv_bias, step_size, log_decay, skip_gain, grad_output):
    tok_rows, channels = conv_input.shape
    heads_here, seq_rows = step_size.shape
    lanes = grad_output.shape[1]
    head_dim = lanes // heads_here
    H = lax.axis_size("head")
    C = lax.axis_size("ctx")
    K = heads_here // GROUP
    W = GROUP * head_dim
    NB = seq_rows // BLOCK
    TPC = W // TILE
    packed = 2 * STATE + 2 * GROUP
    skip = jnp.broadcast_to(jnp.repeat(skip_gain, head_dim)[None, :], (GROUP, lanes))
    dma = pltpu.SemaphoreType.DMA
    vmem = pl.BlockSpec(memory_space=pltpu.VMEM)
    return pl.pallas_call(
        partial(mixer_kernel, H, C, head_dim),
        out_shape=[
            jax.ShapeDtypeStruct((seq_rows, lanes), BF16),
            jax.ShapeDtypeStruct((tok_rows, channels), BF16),
            jax.ShapeDtypeStruct((heads_here, seq_rows), F32),
            jax.ShapeDtypeStruct((heads_here, seq_rows), F32),
        ],
        in_specs=[vmem] * 7,
        out_specs=[vmem] * 4,
        scratch_shapes=[
            pltpu.VMEM((16, channels), BF16),
            pltpu.VMEM((K, H, tok_rows, W), BF16),
            pltpu.VMEM((tok_rows, 2 * STATE), BF16),
            pltpu.VMEM((tok_rows, channels), BF16),
            pltpu.VMEM((K, seq_rows, W), BF16),
            pltpu.VMEM((seq_rows, 2 * STATE), BF16),
            pltpu.VMEM((K, NB, GROUP, BLOCK), F32),
            pltpu.VMEM((NB, BLOCK, BLOCK), F32),
            pltpu.VMEM((NB, BLOCK, BLOCK), F32),
            pltpu.VMEM((K, NB, STATE, W), F32),
            pltpu.VMEM((K, NB, STATE, W), F32),
            pltpu.VMEM((K, NB, GROUP, W), F32),
            pltpu.VMEM((STATE, W), F32),
            pltpu.VMEM((STATE, W), F32),
            pltpu.VMEM((GROUP, W), F32),
            pltpu.VMEM((K, TPC, packed, TILE), BF16),
            pltpu.VMEM((K, C, packed, TILE), BF16),
            pltpu.VMEM((K, C, 2 * STATE, TILE), BF16),
            pltpu.VMEM((K, TPC, 2 * STATE, TILE), BF16),
            pltpu.VMEM((NB, STATE, W), BF16),
            pltpu.VMEM((NB, STATE, W), BF16),
            pltpu.VMEM((NB, GROUP, TILE), F32),
            pltpu.VMEM((K, NB, GROUP, BLOCK), F32),
            pltpu.VMEM((K, NB, GROUP, BLOCK), F32),
            pltpu.VMEM((K, seq_rows, W), BF16),
            pltpu.VMEM((K, H, tok_rows, W), BF16),
            pltpu.VMEM((seq_rows, 2 * STATE), F32),
            pltpu.VMEM((seq_rows, 2 * STATE), BF16),
            pltpu.VMEM((H, tok_rows, 2 * STATE), BF16),
            pltpu.VMEM((K + 1, 8, H * W), F32),
            pltpu.VMEM((K + 1, 8, H * W), F32),
            dma((2,)),
            dma((K, H)),
            dma((K, H)),
            dma((H,)),
            dma((H,)),
            dma((K, TPC)),
            dma((K, C)),
            dma((K, C)),
            dma((K, TPC)),
            dma((K, H)),
            dma((K, H)),
            dma((H,)),
            dma((H,)),
            dma((K + 1,)),
            dma((K + 1,)),
        ],
        compiler_params=pltpu.CompilerParams(
            vmem_limit_bytes=VMEM_LIMIT, collective_id=0, has_side_effects=True
        ),
        cost_estimate=pl.CostEstimate(
            flops=30_000_000_000, bytes_accessed=13_000_000, transcendentals=10_000_000
        ),
        name="mixer",
    )(conv_input, conv_weight, conv_bias[None, :], step_size, log_decay, skip, grad_output)


def solution(mesh):
    return jax.shard_map(
        local,
        mesh=mesh,
        in_specs=(
            P(("ctx", "head"), None),
            P(),
            P(),
            P("head", "ctx"),
            P("head", "ctx"),
            P("head"),
            P("ctx", "head"),
        ),
        out_specs=(P("ctx", "head"), P(("ctx", "head"), None), P("head", "ctx"), P("head", "ctx")),
        check_vma=False,
    )
```

```python
from functools import partial

import jax
import jax.numpy as jnp
from jax import lax
from jax.experimental import pallas as pl
from jax.experimental.pallas import tpu as pltpu
from jax.sharding import PartitionSpec as P

STATE = 128
BLOCK = 256
GROUP = 8
TILE = 128
F32 = jnp.float32
BF16 = jnp.bfloat16
VMEM_LIMIT = 60 * 1024 * 1024
MESH = pl.DeviceIdType.MESH


def dot(a, b, ca, cb):
    return lax.dot_general(
        a, b, (((ca,), (cb,)), ((), ())), preferred_element_type=F32
    )


def head_of_lane(rows, width, head_dim):
    row = lax.broadcasted_iota(jnp.int32, (rows, width), 0)
    lane = lax.broadcasted_iota(jnp.int32, (rows, width), 1)
    return jnp.where(lax.rem(row, GROUP) == lane // head_dim, 1.0, 0.0).astype(BF16)


def expand(rows, width, head_dim):
    high = rows.astype(BF16).astype(F32)
    both = jnp.concatenate([high, rows - high], axis=0).astype(BF16)
    return dot(both, head_of_lane(2 * GROUP, width, head_dim), 0, 0)


def head_sums(value, head_dim):
    pick = head_of_lane(2 * GROUP, value.shape[1], head_dim)
    return dot(pick, value.astype(BF16), 1, 1)[:GROUP]


def triangular(rows, contract):
    length = rows.shape[1]
    row = lax.broadcasted_iota(jnp.int32, (length, length), 0)
    col = lax.broadcasted_iota(jnp.int32, (length, length), 1)
    upper = jnp.where(row <= col, 1.0, 0.0).astype(BF16)
    high = rows.astype(BF16).astype(F32)
    rest = rows - high
    middle = rest.astype(BF16).astype(F32)
    terms = jnp.concatenate([high, middle, rest - middle, jnp.zeros_like(rows)], axis=0)
    sums = dot(terms.astype(BF16), upper, 1, contract)
    return sums[:GROUP] + sums[GROUP : 2 * GROUP] + sums[2 * GROUP : 3 * GROUP]


def at(start, size):
    return pl.ds(pl.multiple_of(start, size), size)


def mixer_kernel(
    H, C, head_dim,
    cin, cw, cb, step, rate, skip, dy,
    y, gin, gs, gd,
    halo, act, actm, dsil, xbuf, mbuf, cums, aff, da, inc, gp, dec,
    t_ref, d_ref, tsend, inbox, outbox, ent, s_ref, g_ref, dots,
    dxbuf, rbuf, acc, gms, gmr, hsend, hrecv,
    halo_send, halo_recv, x_send, x_recv, m_send, m_recv, t_send, t_recv, e_send, e_recv,
    b_send, b_recv, g_send, g_recv, h_send, h_recv,
):
    taps = cw.shape[0]
    TR, channels = cin.shape
    SR, lanes = dy.shape
    K, _, W = xbuf.shape
    NB = SR // BLOCK
    TPC = W // TILE
    inner = H * lanes
    c = lax.axis_index("ctx")
    head = lax.axis_index("head")
    index = c * H + head
    total = C * H
    order = sorted(range(1, H), key=lambda o: abs(o - H // 2))

    def where_is(i):
        return (i // H, i % H)

    following = where_is((index + 1) % total)
    preceding = where_is((index + total - 1) % total)

    barrier = pltpu.get_barrier_semaphore()
    for o in range(1, H):
        pl.semaphore_signal(barrier, inc=1, device_id=(c, (head + o) % H), device_id_type=MESH)
    for o in range(1, C):
        pl.semaphore_signal(barrier, inc=1, device_id=((c + o) % C, head), device_id_type=MESH)
    for who in (following, preceding):
        pl.semaphore_signal(barrier, inc=1, device_id=who, device_id_type=MESH)
    pl.semaphore_wait(barrier, H + C)

    def remote(src, dst, send, recv, who):
        return pltpu.make_async_remote_copy(
            src_ref=src, dst_ref=dst, send_sem=send, recv_sem=recv, device_id=who, device_id_type=MESH
        )

    def send_halo(i, where):
        return remote(
            cin.at[pl.ds(TR - 16, 16), where], halo.at[:, where], halo_send.at[i], halo_recv.at[i], following
        )

    map_lanes = pl.ds(inner, 2 * STATE)

    def chunk_lanes(k, p):
        return at(p * lanes + k * W, W)

    @pl.when(index < total - 1)
    def _():
        send_halo(K * H, map_lanes).start()

        def start_halo(i, carry):
            send_halo(i, chunk_lanes(i // H, i % H)).start()
            return carry

        lax.fori_loop(0, K * H, start_halo, 0)

    @pl.when(index == 0)
    def _():
        halo[...] = jnp.zeros_like(halo)

    @pl.when(index > 0)
    def _():
        send_halo(K * H, map_lanes).wait_recv()

    def convolve(col):
        where = at(col, TILE)
        body = cin[:, where].astype(F32)
        padded = jnp.concatenate([halo[:, where].astype(F32)[8:], body], axis=0)
        first = 8 - (taps - 1)
        pre = cb[pl.ds(col // TILE, 1), :] + cw[0:1, where] * padded[first : first + TR]
        for tap in range(1, taps):
            pre = pre + cw[tap : tap + 1, where] * padded[first + tap : first + tap + TR]
        sig = 0.5 * jnp.tanh(0.5 * pre) + 0.5
        value = pre * sig
        dsil[:, where] = (sig + value * (1.0 - sig)).astype(BF16)
        return value.astype(BF16)

    def peer(o):
        return (head + o) % H

    def source(o):
        return (head + H - o) % H

    def send_maps(o):
        return remote(actm, mbuf.at[at(head * TR, TR)], m_send.at[o], m_recv.at[o], (c, peer(o)))

    def recv_maps(o):
        return remote(actm, mbuf.at[at(source(o) * TR, TR)], m_send.at[o], m_recv.at[o], (c, peer(o)))

    def send_x(k, o):
        return remote(
            act.at[k, peer(o)], xbuf.at[k, at(head * TR, TR)], x_send.at[k, o], x_recv.at[k, o], (c, peer(o))
        )

    def recv_x(k, o):
        return remote(
            act.at[k, peer(o)], xbuf.at[k, at(source(o) * TR, TR)], x_send.at[k, o], x_recv.at[k, o], (c, peer(o))
        )

    for i in range(2 * STATE // TILE):
        actm[:, i * TILE : (i + 1) * TILE] = convolve(inner + i * TILE)
    for o in order:
        send_maps(o).start()
    mbuf[at(head * TR, TR), :] = actm[...]

    def conv_chunk(k, carry):
        @pl.when(index > 0)
        def _():
            for p in range(H):
                send_halo(k * H + p, chunk_lanes(k, p)).wait_recv()

        for o in order + [0]:
            p = peer(o)
            for i in range(TPC):
                value = convolve(p * lanes + k * W + i * TILE)
                if o:
                    act[k, p, :, i * TILE : (i + 1) * TILE] = value
                else:
                    xbuf[k, at(head * TR, TR), i * TILE : (i + 1) * TILE] = value
            if o:
                send_x(k, o).start()
        return carry

    lax.fori_loop(0, K, conv_chunk, 0)

    def sums_chunk(k, carry):
        for b in range(NB):
            cums[k, b] = triangular(rate[at(k * GROUP, GROUP), b * BLOCK : (b + 1) * BLOCK], 0)
        return carry

    lax.fori_loop(0, K, sums_chunk, 0)

    for o in order:
        recv_maps(o).wait_recv()

    row = lax.broadcasted_iota(jnp.int32, (BLOCK, BLOCK), 0)
    col = lax.broadcasted_iota(jnp.int32, (BLOCK, BLOCK), 1)
    causal = row >= col
    for b in range(NB):
        m = mbuf[b * BLOCK : (b + 1) * BLOCK]
        aff[b] = jnp.where(causal, dot(m[:, STATE:], m[:, :STATE], 1, 1), 0.0)
        da[b] = jnp.zeros((BLOCK, BLOCK), F32)
    acc[...] = jnp.zeros_like(acc)

    stride = C // TPC

    def owner(k, j):
        return j * stride + (j + k) % stride

    def send_tile(q, k, j):
        return remote(
            tsend.at[q, k, j], inbox.at[q, k, c], t_send.at[q, k, j], t_recv.at[q, k, c], (owner(k, j), head)
        )

    def recv_tile(q, k, src):
        return remote(tsend.at[q, k, 0], inbox.at[q, k, src], t_send.at[q, k, 0], t_recv.at[q, k, src], (src, head))

    def pass_on(q, k, decay):
        high = decay.astype(BF16).astype(F32)
        both = jnp.concatenate([high, decay - high], axis=0).astype(BF16)
        for j in range(TPC):
            where = slice(j * TILE, (j + 1) * TILE)
            tsend[q, k, j, :STATE] = t_ref[:, where].astype(BF16)
            tsend[q, k, j, STATE:] = both[:, where]
        for j in range(TPC):
            @pl.when(owner(k, j) == c)
            def _():
                inbox[q, k, c] = tsend[q, k, j]

            @pl.when(owner(k, j) != c)
            def _():
                send_tile(q, k, j).start()

    def pulls(k, carry):
        t_ref[...] = jnp.zeros_like(t_ref)
        d_ref[k] = jnp.ones(d_ref.shape[1:], F32)

        def block(b, carry):
            rows = at(b * BLOCK, BLOCK)
            from_start = expand(jnp.exp(cums[k, b]), W, head_dim)
            dyw = (dy[rows, at(k * W, W)].astype(F32) * from_start).astype(BF16)
            grad = dot(mbuf[rows, STATE:], dyw, 0, 0)
            last_dec = from_start[BLOCK - 1 :]
            gp[k, b] = grad
            dec[k, b] = jnp.broadcast_to(last_dec, (GROUP, W))
            t_ref[...] = t_ref[...] + d_ref[k, 0:1] * grad
            d_ref[k] = d_ref[k] * last_dec
            return carry

        lax.fori_loop(0, NB, block, 0)
        pass_on(1, k, d_ref[k])
        return carry

    lax.fori_loop(0, K, pulls, 0)

    def states(k):
        t_ref[...] = jnp.zeros_like(t_ref)

        def block(b, carry):
            rows = at(b * BLOCK, BLOCK)
            cum = cums[k, b]
            to_end = expand(jnp.exp(cum[:, BLOCK - 1 :] - cum) * step[at(k * GROUP, GROUP), rows], W, head_dim)
            xw = (xbuf[k, rows, :].astype(F32) * to_end).astype(BF16)
            more = dot(mbuf[rows, :STATE], xw, 0, 0)
            inc[k, b] = more
            t_ref[...] = t_ref[...] * dec[k, b, 0:1] + more
            return carry

        lax.fori_loop(0, NB, block, 0)
        pass_on(0, k, d_ref[k])

    def send_enter(q, k, j, dst):
        return remote(outbox.at[q, k, dst], ent.at[q, k, j], e_send.at[q, k, dst], e_recv.at[q, k, j], (dst, head))

    def chain(q, k):
        j = c // stride

        @pl.when(c == owner(k, j))
        def _():
            def arrive(src, carry):
                @pl.when(src != c)
                def _():
                    recv_tile(q, k, src).wait_recv()
                return carry

            lax.fori_loop(0, C, arrive, 0)

            def follow(i, state):
                i = C - 1 - i if q else i
                outbox[q, k, i] = state.astype(BF16)
                both = inbox[q, k, i, STATE:].astype(F32)
                return (both[0:1] + both[GROUP : GROUP + 1]) * state + inbox[q, k, i, :STATE].astype(F32)

            lax.fori_loop(0, C, follow, jnp.zeros((STATE, TILE), F32))

            def leave(dst, carry):
                @pl.when(dst != c)
                def _():
                    send_enter(q, k, j, dst).start()
                return carry

            lax.fori_loop(0, C, leave, 0)
            ent[q, k, j] = outbox[q, k, c]

    half = BLOCK // 2
    pair = 2 * head_dim

    def intra(k):
        first = lax.broadcasted_iota(jnp.int32, (half, pair), 1) < head_dim

        def each(value):
            none = jnp.zeros_like(value)
            return jnp.concatenate([jnp.where(first, value, none), jnp.where(first, none, value)], axis=0)

        def block(b, carry):
            rows = at(b * BLOCK, BLOCK)
            cum = cums[k, b]
            cum_col = cum.T
            dyb = dy[rows, at(k * W, W)]
            steps = expand(step[at(k * GROUP, GROUP), rows], W, head_dim)
            xsf = xbuf[k, rows, :].astype(F32) * steps
            xs = xsf.astype(BF16)
            middle = cum[:, half - 1 : half]
            until = expand(jnp.exp(middle - cum[:, :half]), W, head_dim)
            since = expand(jnp.exp(cum[:, half:] - middle), W, head_dim)
            early = (xsf[:half] * until).astype(BF16)
            late = (dyb[half:].astype(F32) * since).astype(BF16)
            across = aff[b, half:, :half].astype(BF16)
            ins_late = since * dot(across, early, 1, 0)
            back_early = until * dot(across, late, 0, 0)
            da[b, half:, :half] += dot(late, early, 1, 1)
            for part in range(2):
                side = slice(part * half, (part + 1) * half)
                near = aff[b, side, side]
                near_da = jnp.zeros((half, half), F32)
                for p in range(GROUP // 2):
                    where = slice(p * pair, (p + 1) * pair)
                    xs_p, dy_p = each(xs[side, where]), dyb[side, where]
                    decays = [
                        jnp.exp(jnp.minimum(cum_col[side, h : h + 1] - cum[h : h + 1, side], 0.0))
                        for h in (2 * p, 2 * p + 1)
                    ]
                    weights = [(near * decay).astype(BF16) for decay in decays]
                    ins = dot(jnp.concatenate(weights, axis=1), xs_p, 1, 0)
                    back = dot(jnp.concatenate(weights, axis=0), each(dy_p), 0, 0)
                    both = dot(dy_p, xs_p, 1, 1)
                    near_da = near_da + both[:, :half] * decays[0] + both[:, half:] * decays[1]
                    if part:
                        ins = ins + ins_late[:, where]
                    else:
                        back = back + back_early[:, where]
                    y[at(b * BLOCK + part * half, half), at(k * W + p * pair, pair)] = ins.astype(BF16)
                    dxbuf[k, at(b * BLOCK + part * half, half), where] = back.astype(BF16)
                da[b, side, side] += near_da
            return carry

        lax.fori_loop(0, NB, block, 0)

    def send_back(k, o):
        return remote(
            dxbuf.at[k, at(peer(o) * TR, TR)], rbuf.at[k, head], b_send.at[k, o], b_recv.at[k, o], (c, peer(o))
        )

    def recv_back(k, o):
        return remote(
            dxbuf.at[k, at(peer(o) * TR, TR)], rbuf.at[k, source(o)], b_send.at[k, o], b_recv.at[k, o], (c, peer(o))
        )

    def carry_over(k):
        for j in range(TPC):
            @pl.when(owner(k, j) != c)
            def _():
                for q in range(2):
                    remote(
                        outbox.at[q, k, 0], ent.at[q, k, j], e_send.at[q, k, 0], e_recv.at[q, k, j], (owner(k, j), head)
                    ).wait_recv()

        state = jnp.concatenate([ent[0, k, j] for j in range(TPC)], axis=1).astype(F32)
        grad = jnp.concatenate([ent[1, k, j] for j in range(TPC)], axis=1).astype(F32)
        grads = [None] * NB
        for b in range(NB - 1, -1, -1):
            grads[b] = grad
            g_ref[b] = grad.astype(BF16)
            if b > 0:
                grad = dec[k, b, 0:1] * grad + gp[k, b]
        for b in range(NB):
            s_ref[b] = state.astype(BF16)
            state = dec[k, b, 0:1] * state + inc[k, b]
            both = jnp.sum(state * grads[b], axis=0, keepdims=True)
            dots[b] = head_sums(jnp.broadcast_to(both, (TILE, W)), head_dim)

        lane_head = lax.broadcasted_iota(jnp.int32, (1, W), 1) // head_dim
        gain = jnp.zeros((1, W), F32)
        for h in range(GROUP):
            gain = jnp.where(lane_head == h, skip[k * GROUP + h], gain)

        def block(turn, carry):
            b = jnp.where(head < H // 2, NB - 1 - turn, turn)
            rows = at(b * BLOCK, BLOCK)
            heads = at(k * GROUP, GROUP)
            wide = at(k * W, W)
            cum = cums[k, b]
            sizes = step[heads, rows]
            from_start = expand(jnp.exp(cum), W, head_dim)
            ending = expand(jnp.exp(cum[:, BLOCK - 1 :] - cum), W, head_dim)
            steps = expand(sizes, W, head_dim)
            x = xbuf[k, rows, :].astype(F32)
            dyf = dy[rows, wide].astype(F32)
            enter, leave = s_ref[b], g_ref[b]
            in_map, out_map = mbuf[rows, :STATE], mbuf[rows, STATE:]
            out = y[rows, wide].astype(F32) + from_start * dot(out_map, enter, 1, 0)
            back = dxbuf[k, rows, :].astype(F32) + ending * dot(in_map, leave, 1, 0)
            y[rows, wide] = (out + gain * x).astype(BF16)
            dxbuf[k, rows, :] = (steps * back + gain * dyf).astype(BF16)
            by_step = head_sums(x * back, head_dim)
            gs[heads, rows] = by_step
            gc = head_sums(dyf * out, head_dim) - sizes * by_step
            place = lax.broadcasted_iota(jnp.int32, gc.shape, 1)
            gc = gc + jnp.where(place == BLOCK - 1, dots[b][:, 0:1], 0.0)
            gd[heads, rows] = triangular(gc, 1)
            acc[rows, :STATE] += dot((x * steps * ending).astype(BF16), leave, 1, 1)
            acc[rows, STATE:] += dot((dyf * from_start).astype(BF16), enter, 1, 1)
            for o in order:
                low, high = peer(o) * TR // BLOCK, (peer(o) * TR + TR - 1) // BLOCK

                @pl.when(b == jnp.where(head < H // 2, low, high))
                def _():
                    send_back(k, o).start()
            return carry

        lax.fori_loop(0, NB, block, 0)
        rbuf[k, head] = dxbuf[k, at(head * TR, TR), :]

    def send_mapgrad(o):
        return remote(gms.at[at(peer(o) * TR, TR)], gmr.at[head], g_send.at[o], g_recv.at[o], (c, peer(o)))

    def recv_mapgrad(o):
        return remote(gms.at[at(peer(o) * TR, TR)], gmr.at[source(o)], g_send.at[o], g_recv.at[o], (c, peer(o)))

    def send_edge(k, wide):
        return remote(
            hsend.at[k, :, pl.ds(0, wide)], hrecv.at[k, :, pl.ds(0, wide)], h_send.at[k], h_recv.at[k], preceding
        )

    def edge(k, wide):
        @pl.when(index > 0)
        def _():
            send_edge(k, wide).start()

    def arrive_edge(k, wide):
        @pl.when(index < total - 1)
        def _():
            send_edge(k, wide).wait_recv()

        @pl.when(index == total - 1)
        def _():
            hrecv[k] = jnp.zeros(hrecv.shape[1:], F32)

    def unwind(grad_pre, tail, where):
        padded = jnp.concatenate([grad_pre, tail], axis=0)
        out = cw[taps - 1 : taps, where] * grad_pre
        for tap in range(taps - 2, -1, -1):
            begin = taps - 1 - tap
            out = out + cw[tap : tap + 1, where] * padded[begin : begin + TR]
        gin[:, where] = out.astype(BF16)

    def first_rows(k):
        for o in order:
            recv_back(k, o).wait_recv()
        for p in range(H):
            where = at(p * lanes + k * W, W)
            top = rbuf[k, p, :16].astype(F32) * dsil[:16, where].astype(F32)
            hsend[k, :, p * W : (p + 1) * W] = top[:8]
        edge(k, H * W)

    def last_rows(k):
        arrive_edge(k, H * W)
        for p in range(H):
            for i in range(TPC):
                where = at(p * lanes + k * W + i * TILE, TILE)
                inside = slice(i * TILE, (i + 1) * TILE)
                grad_pre = rbuf[k, p, :, inside].astype(F32) * dsil[:, where].astype(F32)
                unwind(grad_pre, hrecv[k, :, p * W + i * TILE : p * W + (i + 1) * TILE], where)

    def stage(k, carry):
        @pl.when(k < K)
        def _():
            for o in order:
                recv_x(k, o).wait_recv()
            states(k)
            chain(1, k)
            intra(k)
            chain(0, k)

        @pl.when(k >= 1)
        def _():
            carry_over(k - 1)

        @pl.when(k >= 2)
        def _():
            first_rows(k - 2)

        @pl.when(k >= 3)
        def _():
            last_rows(k - 3)

        return carry

    lax.fori_loop(0, K + 1, stage, 0)

    for b in range(NB):
        rows = slice(b * BLOCK, (b + 1) * BLOCK)
        grad = jnp.where(causal, da[b], 0.0).astype(BF16)
        gms[rows, :STATE] = (acc[rows, :STATE] + dot(grad, mbuf[rows, STATE:], 0, 0)).astype(BF16)
        gms[rows, STATE:] = (acc[rows, STATE:] + dot(grad, mbuf[rows, :STATE], 1, 0)).astype(BF16)
    for o in order:
        send_mapgrad(o).start()
    gmr[head] = gms[at(head * TR, TR), :]

    for k in range(max(K - 2, 0), K - 1):
        last_rows(k)
    first_rows(K - 1)
    for o in order:
        recv_mapgrad(o).wait_recv()
    parts = []
    for i in range(2 * STATE // TILE):
        inside = slice(i * TILE, (i + 1) * TILE)
        summed = gmr[0, :, inside].astype(F32)
        for p in range(1, H):
            summed = summed + gmr[p, :, inside].astype(F32)
        grad_pre = summed.astype(BF16).astype(F32) * dsil[:, inner + i * TILE : inner + (i + 1) * TILE].astype(F32)
        parts.append(grad_pre)
        hsend[K, :, inside] = grad_pre[:8]
    edge(K, 2 * STATE)
    last_rows(K - 1)
    arrive_edge(K, 2 * STATE)
    for i in range(2 * STATE // TILE):
        inside = slice(i * TILE, (i + 1) * TILE)
        unwind(parts[i], hrecv[K, :, inside], slice(inner + i * TILE, inner + (i + 1) * TILE))

    @pl.when(index < total - 1)
    def _():
        send_halo(K * H, map_lanes).wait_send()

        def drain_halo(i, carry):
            send_halo(i, chunk_lanes(i // H, i % H)).wait_send()
            return carry

        lax.fori_loop(0, K * H, drain_halo, 0)

    for o in order:
        send_maps(o).wait_send()
        send_mapgrad(o).wait_send()

    def drain(k, carry):
        for o in order:
            send_x(k, o).wait_send()
            send_back(k, o).wait_send()
        for q in range(2):
            for j in range(TPC):
                @pl.when(owner(k, j) != c)
                def _():
                    send_tile(q, k, j).wait_send()

        @pl.when(c == owner(k, c // stride))
        def _():
            def leave(dst, carry):
                @pl.when(dst != c)
                def _():
                    for q in range(2):
                        send_enter(q, k, c // stride, dst).wait_send()
                return carry

            lax.fori_loop(0, C, leave, 0)

        return carry

    lax.fori_loop(0, K, drain, 0)

    @pl.when(index > 0)
    def _():
        def drain_edges(k, carry):
            send_edge(k, H * W).wait_send()
            return carry

        lax.fori_loop(0, K, drain_edges, 0)
        send_edge(K, 2 * STATE).wait_send()


def local(conv_input, conv_weight, conv_bias, step_size, log_decay, skip_gain, grad_output):
    tok_rows, channels = conv_input.shape
    heads_here, seq_rows = step_size.shape
    lanes = grad_output.shape[1]
    head_dim = lanes // heads_here
    H = lax.axis_size("head")
    C = lax.axis_size("ctx")
    K = heads_here // GROUP
    W = GROUP * head_dim
    NB = seq_rows // BLOCK
    TPC = W // TILE
    packed = STATE + 2 * GROUP
    dma = pltpu.SemaphoreType.DMA
    vmem = pl.BlockSpec(memory_space=pltpu.VMEM)
    return pl.pallas_call(
        partial(mixer_kernel, H, C, head_dim),
        out_shape=[
            jax.ShapeDtypeStruct((seq_rows, lanes), BF16),
            jax.ShapeDtypeStruct((tok_rows, channels), BF16),
            jax.ShapeDtypeStruct((heads_here, seq_rows), F32),
            jax.ShapeDtypeStruct((heads_here, seq_rows), F32),
        ],
        in_specs=[vmem] * 5 + [pl.BlockSpec(memory_space=pltpu.SMEM), vmem],
        out_specs=[vmem] * 4,
        scratch_shapes=[
            pltpu.VMEM((16, channels), BF16),
            pltpu.VMEM((K, H, tok_rows, W), BF16),
            pltpu.VMEM((tok_rows, 2 * STATE), BF16),
            pltpu.VMEM((tok_rows, channels), BF16),
            pltpu.VMEM((K, seq_rows, W), BF16),
            pltpu.VMEM((seq_rows, 2 * STATE), BF16),
            pltpu.VMEM((K, NB, GROUP, BLOCK), F32),
            pltpu.VMEM((NB, BLOCK, BLOCK), F32),
            pltpu.VMEM((NB, BLOCK, BLOCK), F32),
            pltpu.VMEM((K, NB, STATE, W), F32),
            pltpu.VMEM((K, NB, STATE, W), F32),
            pltpu.VMEM((K, NB, GROUP, W), F32),
            pltpu.VMEM((STATE, W), F32),
            pltpu.VMEM((K, GROUP, W), F32),
            pltpu.VMEM((2, K, TPC, packed, TILE), BF16),
            pltpu.VMEM((2, K, C, packed, TILE), BF16),
            pltpu.VMEM((2, K, C, STATE, TILE), BF16),
            pltpu.VMEM((2, K, TPC, STATE, TILE), BF16),
            pltpu.VMEM((NB, STATE, W), BF16),
            pltpu.VMEM((NB, STATE, W), BF16),
            pltpu.VMEM((NB, GROUP, TILE), F32),
            pltpu.VMEM((K, seq_rows, W), BF16),
            pltpu.VMEM((K, H, tok_rows, W), BF16),
            pltpu.VMEM((seq_rows, 2 * STATE), F32),
            pltpu.VMEM((seq_rows, 2 * STATE), BF16),
            pltpu.VMEM((H, tok_rows, 2 * STATE), BF16),
            pltpu.VMEM((K + 1, 8, H * W), F32),
            pltpu.VMEM((K + 1, 8, H * W), F32),
            dma((K * H + 1,)),
            dma((K * H + 1,)),
            dma((K, H)),
            dma((K, H)),
            dma((H,)),
            dma((H,)),
            dma((2, K, TPC)),
            dma((2, K, C)),
            dma((2, K, C)),
            dma((2, K, TPC)),
            dma((K, H)),
            dma((K, H)),
            dma((H,)),
            dma((H,)),
            dma((K + 1,)),
            dma((K + 1,)),
        ],
        compiler_params=pltpu.CompilerParams(
            vmem_limit_bytes=VMEM_LIMIT, collective_id=0, has_side_effects=True
        ),
        cost_estimate=pl.CostEstimate(
            flops=30_000_000_000, bytes_accessed=13_000_000, transcendentals=10_000_000
        ),
        name="mixer",
    )(conv_input, conv_weight, conv_bias.reshape(-1, TILE), step_size, log_decay, skip_gain, grad_output)


def solution(mesh):
    return jax.shard_map(
        local,
        mesh=mesh,
        in_specs=(
            P(("ctx", "head"), None),
            P(),
            P(),
            P("head", "ctx"),
            P("head", "ctx"),
            P("head"),
            P("ctx", "head"),
        ),
        out_specs=(P("ctx", "head"), P(("ctx", "head"), None), P("head", "ctx"), P("head", "ctx")),
        check_vma=False,
    )
```

```python
from functools import partial

import jax
import jax.numpy as jnp
from jax import lax
from jax.experimental import pallas as pl
from jax.experimental.pallas import tpu as pltpu
from jax.sharding import PartitionSpec as P

STATE = 128
BLOCK = 256
GROUP = 8
TILE = 128
F32 = jnp.float32
BF16 = jnp.bfloat16
VMEM_LIMIT = 60 * 1024 * 1024
MESH = pl.DeviceIdType.MESH


def dot(a, b, ca, cb):
    return lax.dot_general(
        a, b, (((ca,), (cb,)), ((), ())), preferred_element_type=F32
    )


def head_of_lane(rows, width, head_dim):
    row = lax.broadcasted_iota(jnp.int32, (rows, width), 0)
    lane = lax.broadcasted_iota(jnp.int32, (rows, width), 1)
    return jnp.where(lax.rem(row, GROUP) == lane // head_dim, 1.0, 0.0).astype(BF16)


def expand(rows, width, head_dim):
    high = rows.astype(BF16).astype(F32)
    both = jnp.concatenate([high, rows - high], axis=0).astype(BF16)
    return dot(both, head_of_lane(2 * GROUP, width, head_dim), 0, 0)


def head_sums(value, head_dim):
    pick = head_of_lane(2 * GROUP, value.shape[1], head_dim)
    return dot(pick, value.astype(BF16), 1, 1)[:GROUP]


def triangular(rows, contract):
    length = rows.shape[1]
    row = lax.broadcasted_iota(jnp.int32, (length, length), 0)
    col = lax.broadcasted_iota(jnp.int32, (length, length), 1)
    upper = jnp.where(row <= col, 1.0, 0.0).astype(BF16)
    high = rows.astype(BF16).astype(F32)
    rest = rows - high
    middle = rest.astype(BF16).astype(F32)
    terms = jnp.concatenate([high, middle, rest - middle, jnp.zeros_like(rows)], axis=0)
    sums = dot(terms.astype(BF16), upper, 1, contract)
    return sums[:GROUP] + sums[GROUP : 2 * GROUP] + sums[2 * GROUP : 3 * GROUP]


def at(start, size):
    return pl.ds(pl.multiple_of(start, size), size)


def mixer_kernel(
    H, C, head_dim,
    cin, cw, cb, step, rate, skip, dy_hbm,
    y_hbm, gin_hbm, gs, gd,
    dy, y, gin, halo, act, actm, dsil, xbuf, mbuf, cums, aff, da, inc, gp, dec,
    t_ref, d_ref, tsend, inbox, outbox, ent, s_ref, g_ref, dots,
    dxbuf, rbuf, acc, gms, gmr, hsend, hrecv,
    dy_sem, y_sem, gin_sem, halo_send, halo_recv, x_send, x_recv, m_send, m_recv, t_send, t_recv, e_send, e_recv,
    b_send, b_recv, g_send, g_recv, h_send, h_recv,
):
    taps = cw.shape[0]
    TR, channels = cin.shape
    SR, lanes = dy.shape
    K, _, W = xbuf.shape
    NB = SR // BLOCK
    TPC = W // TILE
    inner = H * lanes
    c = lax.axis_index("ctx")
    head = lax.axis_index("head")
    index = c * H + head
    total = C * H
    order = sorted(range(1, H), key=lambda o: abs(o - H // 2))

    def where_is(i):
        return (i // H, i % H)

    following = where_is((index + 1) % total)
    preceding = where_is((index + total - 1) % total)

    dy_copy = pltpu.make_async_copy(dy_hbm, dy, dy_sem)
    dy_copy.start()
    barrier = pltpu.get_barrier_semaphore()
    for o in range(1, H):
        pl.semaphore_signal(barrier, inc=1, device_id=(c, (head + o) % H), device_id_type=MESH)
    for o in range(1, C):
        pl.semaphore_signal(barrier, inc=1, device_id=((c + o) % C, head), device_id_type=MESH)
    for who in (following, preceding):
        pl.semaphore_signal(barrier, inc=1, device_id=who, device_id_type=MESH)
    pl.semaphore_wait(barrier, H + C)

    def remote(src, dst, send, recv, who):
        return pltpu.make_async_remote_copy(
            src_ref=src, dst_ref=dst, send_sem=send, recv_sem=recv, device_id=who, device_id_type=MESH
        )

    def send_halo(i, where):
        return remote(
            cin.at[pl.ds(TR - 16, 16), where], halo.at[:, where], halo_send.at[i], halo_recv.at[i], following
        )

    map_lanes = pl.ds(inner, 2 * STATE)

    def chunk_lanes(k, p):
        return at(p * lanes + k * W, W)

    @pl.when(index < total - 1)
    def _():
        send_halo(K * H, map_lanes).start()

        def start_halo(i, carry):
            send_halo(i, chunk_lanes(i // H, i % H)).start()
            return carry

        lax.fori_loop(0, K * H, start_halo, 0)

    @pl.when(index == 0)
    def _():
        halo[...] = jnp.zeros_like(halo)

    @pl.when(index > 0)
    def _():
        send_halo(K * H, map_lanes).wait_recv()

    def convolve(col):
        where = at(col, TILE)
        body = cin[:, where].astype(F32)
        padded = jnp.concatenate([halo[:, where].astype(F32)[8:], body], axis=0)
        first = 8 - (taps - 1)
        pre = cb[pl.ds(col // TILE, 1), :] + cw[0:1, where] * padded[first : first + TR]
        for tap in range(1, taps):
            pre = pre + cw[tap : tap + 1, where] * padded[first + tap : first + tap + TR]
        sig = 0.5 * jnp.tanh(0.5 * pre) + 0.5
        value = pre * sig
        dsil[:, where] = (sig + value * (1.0 - sig)).astype(BF16)
        return value.astype(BF16)

    def peer(o):
        return (head + o) % H

    def source(o):
        return (head + H - o) % H

    def send_maps(o):
        return remote(actm, mbuf.at[at(head * TR, TR)], m_send.at[o], m_recv.at[o], (c, peer(o)))

    def recv_maps(o):
        return remote(actm, mbuf.at[at(source(o) * TR, TR)], m_send.at[o], m_recv.at[o], (c, peer(o)))

    def send_x(k, o):
        return remote(
            act.at[k, peer(o)], xbuf.at[k, at(head * TR, TR)], x_send.at[k, o], x_recv.at[k, o], (c, peer(o))
        )

    def recv_x(k, o):
        return remote(
            act.at[k, peer(o)], xbuf.at[k, at(source(o) * TR, TR)], x_send.at[k, o], x_recv.at[k, o], (c, peer(o))
        )

    for i in range(2 * STATE // TILE):
        actm[:, i * TILE : (i + 1) * TILE] = convolve(inner + i * TILE)
    for o in order:
        send_maps(o).start()
    mbuf[at(head * TR, TR), :] = actm[...]

    def conv_chunk(k, carry):
        @pl.when(index > 0)
        def _():
            for p in range(H):
                send_halo(k * H + p, chunk_lanes(k, p)).wait_recv()

        for o in order + [0]:
            p = peer(o)
            for i in range(TPC):
                value = convolve(p * lanes + k * W + i * TILE)
                if o:
                    act[k, p, :, i * TILE : (i + 1) * TILE] = value
                else:
                    xbuf[k, at(head * TR, TR), i * TILE : (i + 1) * TILE] = value
            if o:
                send_x(k, o).start()
        return carry

    lax.fori_loop(0, K, conv_chunk, 0)

    def sums_chunk(k, carry):
        for b in range(NB):
            cums[k, b] = triangular(rate[at(k * GROUP, GROUP), b * BLOCK : (b + 1) * BLOCK], 0)
        return carry

    lax.fori_loop(0, K, sums_chunk, 0)

    for o in order:
        recv_maps(o).wait_recv()

    row = lax.broadcasted_iota(jnp.int32, (BLOCK, BLOCK), 0)
    col = lax.broadcasted_iota(jnp.int32, (BLOCK, BLOCK), 1)
    causal = row >= col
    for b in range(NB):
        m = mbuf[b * BLOCK : (b + 1) * BLOCK]
        aff[b] = jnp.where(causal, dot(m[:, STATE:], m[:, :STATE], 1, 1), 0.0)
        da[b] = jnp.zeros((BLOCK, BLOCK), F32)
    acc[...] = jnp.zeros_like(acc)

    stride = C // TPC

    def owner(k, j):
        return j * stride + (j + k) % stride

    def send_tile(q, k, j):
        return remote(
            tsend.at[q, k, j], inbox.at[q, k, c], t_send.at[q, k, j], t_recv.at[q, k, c], (owner(k, j), head)
        )

    def recv_tile(q, k, src):
        return remote(tsend.at[q, k, 0], inbox.at[q, k, src], t_send.at[q, k, 0], t_recv.at[q, k, src], (src, head))

    def pass_on(q, k, decay):
        high = decay.astype(BF16).astype(F32)
        both = jnp.concatenate([high, decay - high], axis=0).astype(BF16)
        for j in range(TPC):
            where = slice(j * TILE, (j + 1) * TILE)
            tsend[q, k, j, :STATE] = t_ref[:, where].astype(BF16)
            tsend[q, k, j, STATE:] = both[:, where]
        for j in range(TPC):
            @pl.when(owner(k, j) == c)
            def _():
                inbox[q, k, c] = tsend[q, k, j]

            @pl.when(owner(k, j) != c)
            def _():
                send_tile(q, k, j).start()

    def pulls(k, carry):
        t_ref[...] = jnp.zeros_like(t_ref)
        d_ref[k] = jnp.ones(d_ref.shape[1:], F32)

        def block(b, carry):
            rows = at(b * BLOCK, BLOCK)
            from_start = expand(jnp.exp(cums[k, b]), W, head_dim)
            dyw = (dy[rows, at(k * W, W)].astype(F32) * from_start).astype(BF16)
            grad = dot(mbuf[rows, STATE:], dyw, 0, 0)
            last_dec = from_start[BLOCK - 1 :]
            gp[k, b] = grad
            dec[k, b] = jnp.broadcast_to(last_dec, (GROUP, W))
            t_ref[...] = t_ref[...] + d_ref[k, 0:1] * grad
            d_ref[k] = d_ref[k] * last_dec
            return carry

        lax.fori_loop(0, NB, block, 0)
        pass_on(1, k, d_ref[k])
        return carry

    dy_copy.wait()
    lax.fori_loop(0, K, pulls, 0)

    def states(k):
        t_ref[...] = jnp.zeros_like(t_ref)

        def block(b, carry):
            rows = at(b * BLOCK, BLOCK)
            cum = cums[k, b]
            to_end = expand(jnp.exp(cum[:, BLOCK - 1 :] - cum) * step[at(k * GROUP, GROUP), rows], W, head_dim)
            xw = (xbuf[k, rows, :].astype(F32) * to_end).astype(BF16)
            more = dot(mbuf[rows, :STATE], xw, 0, 0)
            inc[k, b] = more
            t_ref[...] = t_ref[...] * dec[k, b, 0:1] + more
            return carry

        lax.fori_loop(0, NB, block, 0)
        pass_on(0, k, d_ref[k])

    def send_enter(q, k, j, dst):
        return remote(outbox.at[q, k, dst], ent.at[q, k, j], e_send.at[q, k, dst], e_recv.at[q, k, j], (dst, head))

    def chain(q, k):
        j = c // stride

        @pl.when(c == owner(k, j))
        def _():
            def arrive(src, carry):
                @pl.when(src != c)
                def _():
                    recv_tile(q, k, src).wait_recv()
                return carry

            lax.fori_loop(0, C, arrive, 0)

            def follow(i, state):
                i = C - 1 - i if q else i
                outbox[q, k, i] = state.astype(BF16)
                both = inbox[q, k, i, STATE:].astype(F32)
                return (both[0:1] + both[GROUP : GROUP + 1]) * state + inbox[q, k, i, :STATE].astype(F32)

            lax.fori_loop(0, C, follow, jnp.zeros((STATE, TILE), F32))

            def leave(dst, carry):
                @pl.when(dst != c)
                def _():
                    send_enter(q, k, j, dst).start()
                return carry

            lax.fori_loop(0, C, leave, 0)
            ent[q, k, j] = outbox[q, k, c]

    half = BLOCK // 2
    pair = 2 * head_dim

    def intra(k):
        first = lax.broadcasted_iota(jnp.int32, (half, pair), 1) < head_dim

        def each(value):
            none = jnp.zeros_like(value)
            return jnp.concatenate([jnp.where(first, value, none), jnp.where(first, none, value)], axis=0)

        def block(b, carry):
            rows = at(b * BLOCK, BLOCK)
            cum = cums[k, b]
            cum_col = cum.T
            dyb = dy[rows, at(k * W, W)]
            steps = expand(step[at(k * GROUP, GROUP), rows], W, head_dim)
            xsf = xbuf[k, rows, :].astype(F32) * steps
            xs = xsf.astype(BF16)
            middle = cum[:, half - 1 : half]
            until = expand(jnp.exp(middle - cum[:, :half]), W, head_dim)
            since = expand(jnp.exp(cum[:, half:] - middle), W, head_dim)
            early = (xsf[:half] * until).astype(BF16)
            late = (dyb[half:].astype(F32) * since).astype(BF16)
            across = aff[b, half:, :half].astype(BF16)
            ins_late = since * dot(across, early, 1, 0)
            back_early = until * dot(across, late, 0, 0)
            da[b, half:, :half] += dot(late, early, 1, 1)
            for part in range(2):
                side = slice(part * half, (part + 1) * half)
                near = aff[b, side, side]
                near_da = jnp.zeros((half, half), F32)
                for p in range(GROUP // 2):
                    where = slice(p * pair, (p + 1) * pair)
                    xs_p, dy_p = each(xs[side, where]), dyb[side, where]
                    decays = [
                        jnp.exp(jnp.minimum(cum_col[side, h : h + 1] - cum[h : h + 1, side], 0.0))
                        for h in (2 * p, 2 * p + 1)
                    ]
                    weights = [(near * decay).astype(BF16) for decay in decays]
                    ins = dot(jnp.concatenate(weights, axis=1), xs_p, 1, 0)
                    back = dot(jnp.concatenate(weights, axis=0), each(dy_p), 0, 0)
                    both = dot(dy_p, xs_p, 1, 1)
                    near_da = near_da + both[:, :half] * decays[0] + both[:, half:] * decays[1]
                    if part:
                        ins = ins + ins_late[:, where]
                    else:
                        back = back + back_early[:, where]
                    y[at(b * BLOCK + part * half, half), at(k * W + p * pair, pair)] = ins.astype(BF16)
                    dxbuf[k, at(b * BLOCK + part * half, half), where] = back.astype(BF16)
                da[b, side, side] += near_da
            return carry

        lax.fori_loop(0, NB, block, 0)

    def send_back(k, o):
        return remote(
            dxbuf.at[k, at(peer(o) * TR, TR)], rbuf.at[k, head], b_send.at[k, o], b_recv.at[k, o], (c, peer(o))
        )

    def recv_back(k, o):
        return remote(
            dxbuf.at[k, at(peer(o) * TR, TR)], rbuf.at[k, source(o)], b_send.at[k, o], b_recv.at[k, o], (c, peer(o))
        )

    def store_y(k):
        wide = at(k * W, W)
        return pltpu.make_async_copy(y.at[:, wide], y_hbm.at[:, wide], y_sem.at[k])

    def store_gin(i, where):
        return pltpu.make_async_copy(gin.at[:, where], gin_hbm.at[:, where], gin_sem.at[i])

    def carry_over(k):
        for j in range(TPC):
            @pl.when(owner(k, j) != c)
            def _():
                for q in range(2):
                    remote(
                        outbox.at[q, k, 0], ent.at[q, k, j], e_send.at[q, k, 0], e_recv.at[q, k, j], (owner(k, j), head)
                    ).wait_recv()

        state = jnp.concatenate([ent[0, k, j] for j in range(TPC)], axis=1).astype(F32)
        grad = jnp.concatenate([ent[1, k, j] for j in range(TPC)], axis=1).astype(F32)
        grads = [None] * NB
        for b in range(NB - 1, -1, -1):
            grads[b] = grad
            g_ref[b] = grad.astype(BF16)
            if b > 0:
                grad = dec[k, b, 0:1] * grad + gp[k, b]
        for b in range(NB):
            s_ref[b] = state.astype(BF16)
            state = dec[k, b, 0:1] * state + inc[k, b]
            both = jnp.sum(state * grads[b], axis=0, keepdims=True)
            dots[b] = head_sums(jnp.broadcast_to(both, (TILE, W)), head_dim)

        lane_head = lax.broadcasted_iota(jnp.int32, (1, W), 1) // head_dim
        gain = jnp.zeros((1, W), F32)
        for h in range(GROUP):
            gain = jnp.where(lane_head == h, skip[k * GROUP + h], gain)

        def block(turn, carry):
            b = jnp.where(head < H // 2, NB - 1 - turn, turn)
            rows = at(b * BLOCK, BLOCK)
            heads = at(k * GROUP, GROUP)
            wide = at(k * W, W)
            cum = cums[k, b]
            sizes = step[heads, rows]
            from_start = expand(jnp.exp(cum), W, head_dim)
            ending = expand(jnp.exp(cum[:, BLOCK - 1 :] - cum), W, head_dim)
            steps = expand(sizes, W, head_dim)
            x = xbuf[k, rows, :].astype(F32)
            dyf = dy[rows, wide].astype(F32)
            enter, leave = s_ref[b], g_ref[b]
            in_map, out_map = mbuf[rows, :STATE], mbuf[rows, STATE:]
            out = y[rows, wide].astype(F32) + from_start * dot(out_map, enter, 1, 0)
            back = dxbuf[k, rows, :].astype(F32) + ending * dot(in_map, leave, 1, 0)
            y[rows, wide] = (out + gain * x).astype(BF16)
            dxbuf[k, rows, :] = (steps * back + gain * dyf).astype(BF16)
            by_step = head_sums(x * back, head_dim)
            gs[heads, rows] = by_step
            gc = head_sums(dyf * out, head_dim) - sizes * by_step
            place = lax.broadcasted_iota(jnp.int32, gc.shape, 1)
            gc = gc + jnp.where(place == BLOCK - 1, dots[b][:, 0:1], 0.0)
            gd[heads, rows] = triangular(gc, 1)
            acc[rows, :STATE] += dot((x * steps * ending).astype(BF16), leave, 1, 1)
            acc[rows, STATE:] += dot((dyf * from_start).astype(BF16), enter, 1, 1)
            for o in order:
                low, high = peer(o) * TR // BLOCK, (peer(o) * TR + TR - 1) // BLOCK

                @pl.when(b == jnp.where(head < H // 2, low, high))
                def _():
                    send_back(k, o).start()
            return carry

        lax.fori_loop(0, NB, block, 0)
        store_y(k).start()
        rbuf[k, head] = dxbuf[k, at(head * TR, TR), :]

    def send_mapgrad(o):
        return remote(gms.at[at(peer(o) * TR, TR)], gmr.at[head], g_send.at[o], g_recv.at[o], (c, peer(o)))

    def recv_mapgrad(o):
        return remote(gms.at[at(peer(o) * TR, TR)], gmr.at[source(o)], g_send.at[o], g_recv.at[o], (c, peer(o)))

    def send_edge(k, wide):
        return remote(
            hsend.at[k, :, pl.ds(0, wide)], hrecv.at[k, :, pl.ds(0, wide)], h_send.at[k], h_recv.at[k], preceding
        )

    def edge(k, wide):
        @pl.when(index > 0)
        def _():
            send_edge(k, wide).start()

    def arrive_edge(k, wide):
        @pl.when(index < total - 1)
        def _():
            send_edge(k, wide).wait_recv()

        @pl.when(index == total - 1)
        def _():
            hrecv[k] = jnp.zeros(hrecv.shape[1:], F32)

    def unwind(grad_pre, tail, where):
        padded = jnp.concatenate([grad_pre, tail], axis=0)
        out = cw[taps - 1 : taps, where] * grad_pre
        for tap in range(taps - 2, -1, -1):
            begin = taps - 1 - tap
            out = out + cw[tap : tap + 1, where] * padded[begin : begin + TR]
        gin[:, where] = out.astype(BF16)

    def first_rows(k):
        for o in order:
            recv_back(k, o).wait_recv()
        for p in range(H):
            where = at(p * lanes + k * W, W)
            top = rbuf[k, p, :16].astype(F32) * dsil[:16, where].astype(F32)
            hsend[k, :, p * W : (p + 1) * W] = top[:8]
        edge(k, H * W)

    def last_rows(k):
        arrive_edge(k, H * W)
        for p in range(H):
            for i in range(TPC):
                where = at(p * lanes + k * W + i * TILE, TILE)
                inside = slice(i * TILE, (i + 1) * TILE)
                grad_pre = rbuf[k, p, :, inside].astype(F32) * dsil[:, where].astype(F32)
                unwind(grad_pre, hrecv[k, :, p * W + i * TILE : p * W + (i + 1) * TILE], where)
            store_gin(k * H + p, chunk_lanes(k, p)).start()

    def stage(k, carry):
        @pl.when(k < K)
        def _():
            for o in order:
                recv_x(k, o).wait_recv()
            states(k)
            chain(1, k)
            intra(k)
            chain(0, k)

        @pl.when(k >= 1)
        def _():
            carry_over(k - 1)

        @pl.when(k >= 2)
        def _():
            first_rows(k - 2)

        @pl.when(k >= 3)
        def _():
            last_rows(k - 3)

        return carry

    lax.fori_loop(0, K + 1, stage, 0)

    for b in range(NB):
        rows = slice(b * BLOCK, (b + 1) * BLOCK)
        grad = jnp.where(causal, da[b], 0.0).astype(BF16)
        gms[rows, :STATE] = (acc[rows, :STATE] + dot(grad, mbuf[rows, STATE:], 0, 0)).astype(BF16)
        gms[rows, STATE:] = (acc[rows, STATE:] + dot(grad, mbuf[rows, :STATE], 1, 0)).astype(BF16)
    for o in order:
        send_mapgrad(o).start()
    gmr[head] = gms[at(head * TR, TR), :]

    for k in range(max(K - 2, 0), K - 1):
        last_rows(k)
    first_rows(K - 1)
    for o in order:
        recv_mapgrad(o).wait_recv()
    parts = []
    for i in range(2 * STATE // TILE):
        inside = slice(i * TILE, (i + 1) * TILE)
        summed = gmr[0, :, inside].astype(F32)
        for p in range(1, H):
            summed = summed + gmr[p, :, inside].astype(F32)
        grad_pre = summed.astype(BF16).astype(F32) * dsil[:, inner + i * TILE : inner + (i + 1) * TILE].astype(F32)
        parts.append(grad_pre)
        hsend[K, :, inside] = grad_pre[:8]
    edge(K, 2 * STATE)
    last_rows(K - 1)
    arrive_edge(K, 2 * STATE)
    for i in range(2 * STATE // TILE):
        inside = slice(i * TILE, (i + 1) * TILE)
        unwind(parts[i], hrecv[K, :, inside], slice(inner + i * TILE, inner + (i + 1) * TILE))

    store_gin(K * H, map_lanes).start()

    @pl.when(index < total - 1)
    def _():
        send_halo(K * H, map_lanes).wait_send()

        def drain_halo(i, carry):
            send_halo(i, chunk_lanes(i // H, i % H)).wait_send()
            return carry

        lax.fori_loop(0, K * H, drain_halo, 0)

    for o in order:
        send_maps(o).wait_send()
        send_mapgrad(o).wait_send()

    def drain(k, carry):
        for o in order:
            send_x(k, o).wait_send()
            send_back(k, o).wait_send()
        for q in range(2):
            for j in range(TPC):
                @pl.when(owner(k, j) != c)
                def _():
                    send_tile(q, k, j).wait_send()

        @pl.when(c == owner(k, c // stride))
        def _():
            def leave(dst, carry):
                @pl.when(dst != c)
                def _():
                    for q in range(2):
                        send_enter(q, k, c // stride, dst).wait_send()
                return carry

            lax.fori_loop(0, C, leave, 0)

        return carry

    lax.fori_loop(0, K, drain, 0)

    def stored(k, carry):
        store_y(k).wait()
        for p in range(H):
            store_gin(k * H + p, chunk_lanes(k, p)).wait()
        return carry

    lax.fori_loop(0, K, stored, 0)
    store_gin(K * H, map_lanes).wait()

    @pl.when(index > 0)
    def _():
        def drain_edges(k, carry):
            send_edge(k, H * W).wait_send()
            return carry

        lax.fori_loop(0, K, drain_edges, 0)
        send_edge(K, 2 * STATE).wait_send()


def hand_on_kernel(count, *refs):
    ins, outs, held = refs[:count], refs[count : 2 * count], refs[2 * count : 3 * count]
    in_sem, out_sem = refs[3 * count :]
    loads, stores = [], []
    for source, target, keep in zip(ins, outs, held):
        rows = source.shape[0]
        pieces = 6 if rows % 96 == 0 else 1
        for i in range(pieces):
            part = pl.ds(i * (rows // pieces), rows // pieces)
            loads.append(pltpu.make_async_copy(source.at[part], keep.at[part], in_sem.at[len(loads)]))
            stores.append(pltpu.make_async_copy(keep.at[part], target.at[part], out_sem.at[len(stores)]))
    for load in loads:
        load.start()
    for load, store in zip(loads, stores):
        load.wait()
        store.start()
    for store in stores:
        store.wait()


def hand_on(arrays):
    anywhere = pl.BlockSpec(memory_space=pl.ANY)
    count = len(arrays)
    return pl.pallas_call(
        partial(hand_on_kernel, count),
        out_shape=[jax.ShapeDtypeStruct(a.shape, a.dtype) for a in arrays],
        in_specs=[anywhere] * count,
        out_specs=[anywhere] * count,
        scratch_shapes=[pltpu.VMEM(a.shape, a.dtype) for a in arrays]
        + [pltpu.SemaphoreType.DMA((6 * count,))] * 2,
        compiler_params=pltpu.CompilerParams(vmem_limit_bytes=VMEM_LIMIT),
        name="hand_on",
    )(*arrays)


def local(conv_input, conv_weight, conv_bias, step_size, log_decay, skip_gain, grad_output):
    tok_rows, channels = conv_input.shape
    heads_here, seq_rows = step_size.shape
    lanes = grad_output.shape[1]
    head_dim = lanes // heads_here
    H = lax.axis_size("head")
    C = lax.axis_size("ctx")
    K = heads_here // GROUP
    W = GROUP * head_dim
    NB = seq_rows // BLOCK
    TPC = W // TILE
    packed = STATE + 2 * GROUP
    dma = pltpu.SemaphoreType.DMA
    vmem = pl.BlockSpec(memory_space=pltpu.VMEM)
    results = pl.pallas_call(
        partial(mixer_kernel, H, C, head_dim),
        out_shape=[
            jax.ShapeDtypeStruct((seq_rows, lanes), BF16),
            jax.ShapeDtypeStruct((tok_rows, channels), BF16),
            jax.ShapeDtypeStruct((heads_here, seq_rows), F32),
            jax.ShapeDtypeStruct((heads_here, seq_rows), F32),
        ],
        in_specs=[vmem] * 5 + [pl.BlockSpec(memory_space=pltpu.SMEM), pl.BlockSpec(memory_space=pl.ANY)],
        out_specs=[pl.BlockSpec(memory_space=pl.ANY)] * 2 + [vmem] * 2,
        scratch_shapes=[
            pltpu.VMEM((seq_rows, lanes), BF16),
            pltpu.VMEM((seq_rows, lanes), BF16),
            pltpu.VMEM((tok_rows, channels), BF16),
            pltpu.VMEM((16, channels), BF16),
            pltpu.VMEM((K, H, tok_rows, W), BF16),
            pltpu.VMEM((tok_rows, 2 * STATE), BF16),
            pltpu.VMEM((tok_rows, channels), BF16),
            pltpu.VMEM((K, seq_rows, W), BF16),
            pltpu.VMEM((seq_rows, 2 * STATE), BF16),
            pltpu.VMEM((K, NB, GROUP, BLOCK), F32),
            pltpu.VMEM((NB, BLOCK, BLOCK), F32),
            pltpu.VMEM((NB, BLOCK, BLOCK), F32),
            pltpu.VMEM((K, NB, STATE, W), F32),
            pltpu.VMEM((K, NB, STATE, W), F32),
            pltpu.VMEM((K, NB, GROUP, W), F32),
            pltpu.VMEM((STATE, W), F32),
            pltpu.VMEM((K, GROUP, W), F32),
            pltpu.VMEM((2, K, TPC, packed, TILE), BF16),
            pltpu.VMEM((2, K, C, packed, TILE), BF16),
            pltpu.VMEM((2, K, C, STATE, TILE), BF16),
            pltpu.VMEM((2, K, TPC, STATE, TILE), BF16),
            pltpu.VMEM((NB, STATE, W), BF16),
            pltpu.VMEM((NB, STATE, W), BF16),
            pltpu.VMEM((NB, GROUP, TILE), F32),
            pltpu.VMEM((K, seq_rows, W), BF16),
            pltpu.VMEM((K, H, tok_rows, W), BF16),
            pltpu.VMEM((seq_rows, 2 * STATE), F32),
            pltpu.VMEM((seq_rows, 2 * STATE), BF16),
            pltpu.VMEM((H, tok_rows, 2 * STATE), BF16),
            pltpu.VMEM((K + 1, 8, H * W), F32),
            pltpu.VMEM((K + 1, 8, H * W), F32),
            dma,
            dma((K,)),
            dma((K * H + 1,)),
            dma((K * H + 1,)),
            dma((K * H + 1,)),
            dma((K, H)),
            dma((K, H)),
            dma((H,)),
            dma((H,)),
            dma((2, K, TPC)),
            dma((2, K, C)),
            dma((2, K, C)),
            dma((2, K, TPC)),
            dma((K, H)),
            dma((K, H)),
            dma((H,)),
            dma((H,)),
            dma((K + 1,)),
            dma((K + 1,)),
        ],
        compiler_params=pltpu.CompilerParams(
            vmem_limit_bytes=VMEM_LIMIT, collective_id=0, has_side_effects=True
        ),
        cost_estimate=pl.CostEstimate(
            flops=30_000_000_000, bytes_accessed=13_000_000, transcendentals=10_000_000
        ),
        name="mixer",
    )(conv_input, conv_weight, conv_bias.reshape(-1, TILE), step_size, log_decay, skip_gain, grad_output)
    return tuple(hand_on(results))


def solution(mesh):
    return jax.shard_map(
        local,
        mesh=mesh,
        in_specs=(
            P(("ctx", "head"), None),
            P(),
            P(),
            P("head", "ctx"),
            P("head", "ctx"),
            P("head"),
            P("ctx", "head"),
        ),
        out_specs=(P("ctx", "head"), P(("ctx", "head"), None), P("head", "ctx"), P("head", "ctx")),
        check_vma=False,
    )
```

```python
from functools import partial

import jax
import jax.numpy as jnp
from jax import lax
from jax.experimental import pallas as pl
from jax.experimental.pallas import tpu as pltpu
from jax.sharding import PartitionSpec as P

STATE = 128
BLOCK = 256
GROUP = 8
TILE = 128
F32 = jnp.float32
BF16 = jnp.bfloat16
VMEM_LIMIT = 60 * 1024 * 1024
MESH = pl.DeviceIdType.MESH


def dot(a, b, ca, cb):
    return lax.dot_general(
        a, b, (((ca,), (cb,)), ((), ())), preferred_element_type=F32
    )


def head_of_lane(rows, width, head_dim):
    row = lax.broadcasted_iota(jnp.int32, (rows, width), 0)
    lane = lax.broadcasted_iota(jnp.int32, (rows, width), 1)
    return jnp.where(lax.rem(row, GROUP) == lane // head_dim, 1.0, 0.0).astype(BF16)


def expand(rows, width, head_dim):
    high = rows.astype(BF16).astype(F32)
    both = jnp.concatenate([high, rows - high], axis=0).astype(BF16)
    return dot(both, head_of_lane(2 * GROUP, width, head_dim), 0, 0)


def head_sums(value, head_dim):
    pick = head_of_lane(2 * GROUP, value.shape[1], head_dim)
    return dot(pick, value.astype(BF16), 1, 1)[:GROUP]


def triangular(rows, contract):
    length = rows.shape[1]
    row = lax.broadcasted_iota(jnp.int32, (length, length), 0)
    col = lax.broadcasted_iota(jnp.int32, (length, length), 1)
    upper = jnp.where(row <= col, 1.0, 0.0).astype(BF16)
    high = rows.astype(BF16).astype(F32)
    rest = rows - high
    middle = rest.astype(BF16).astype(F32)
    terms = jnp.concatenate([high, middle, rest - middle, jnp.zeros_like(rows)], axis=0)
    sums = dot(terms.astype(BF16), upper, 1, contract)
    return sums[:GROUP] + sums[GROUP : 2 * GROUP] + sums[2 * GROUP : 3 * GROUP]


def at(start, size):
    return pl.ds(pl.multiple_of(start, size), size)


def mixer_kernel(
    H, C, head_dim,
    cin, cw, cb, step, rate, skip, dy_hbm,
    y_hbm, gin_hbm, gs, gd,
    dy, y, gin, halo, act, actm, dsil, xbuf, mbuf, cums, aff, da, inc, gp, dec,
    t_ref, d_ref, tsend, inbox, outbox, ent, s_ref, g_ref, dots,
    dxbuf, rbuf, acc, gms, gmr, hsend, hrecv,
    dy_sem, y_sem, gin_sem, halo_send, halo_recv, x_send, x_recv, m_send, m_recv, t_send, t_recv, e_send, e_recv,
    b_send, b_recv, g_send, g_recv, h_send, h_recv,
):
    taps = cw.shape[0]
    TR, channels = cin.shape
    SR, lanes = dy.shape
    K, _, W = xbuf.shape
    NB = SR // BLOCK
    TPC = W // TILE
    inner = H * lanes
    c = lax.axis_index("ctx")
    head = lax.axis_index("head")
    index = c * H + head
    total = C * H
    order = sorted(range(1, H), key=lambda o: abs(o - H // 2))

    def where_is(i):
        return (i // H, i % H)

    following = where_is((index + 1) % total)
    preceding = where_is((index + total - 1) % total)

    dy_copy = pltpu.make_async_copy(dy_hbm, dy, dy_sem)
    dy_copy.start()
    barrier = pltpu.get_barrier_semaphore()
    for o in range(1, H):
        pl.semaphore_signal(barrier, inc=1, device_id=(c, (head + o) % H), device_id_type=MESH)
    for o in range(1, C):
        pl.semaphore_signal(barrier, inc=1, device_id=((c + o) % C, head), device_id_type=MESH)
    for who in (following, preceding):
        pl.semaphore_signal(barrier, inc=1, device_id=who, device_id_type=MESH)
    pl.semaphore_wait(barrier, H + C)

    def remote(src, dst, send, recv, who):
        return pltpu.make_async_remote_copy(
            src_ref=src, dst_ref=dst, send_sem=send, recv_sem=recv, device_id=who, device_id_type=MESH
        )

    def send_halo(i, where):
        return remote(
            cin.at[pl.ds(TR - 16, 16), where], halo.at[:, where], halo_send.at[i], halo_recv.at[i], following
        )

    map_lanes = pl.ds(inner, 2 * STATE)

    def chunk_lanes(k, p):
        return at(p * lanes + k * W, W)

    @pl.when(index < total - 1)
    def _():
        send_halo(K * H, map_lanes).start()

        def start_halo(i, carry):
            send_halo(i, chunk_lanes(i // H, i % H)).start()
            return carry

        lax.fori_loop(0, K * H, start_halo, 0)

    @pl.when(index == 0)
    def _():
        halo[...] = jnp.zeros_like(halo)

    @pl.when(index > 0)
    def _():
        send_halo(K * H, map_lanes).wait_recv()

    def convolve(col):
        where = at(col, TILE)
        body = cin[:, where].astype(F32)
        padded = jnp.concatenate([halo[:, where].astype(F32)[8:], body], axis=0)
        first = 8 - (taps - 1)
        pre = cb[pl.ds(col // TILE, 1), :] + cw[0:1, where] * padded[first : first + TR]
        for tap in range(1, taps):
            pre = pre + cw[tap : tap + 1, where] * padded[first + tap : first + tap + TR]
        sig = 0.5 * jnp.tanh(0.5 * pre) + 0.5
        value = pre * sig
        dsil[:, where] = (sig + value * (1.0 - sig)).astype(BF16)
        return value.astype(BF16)

    def peer(o):
        return (head + o) % H

    def source(o):
        return (head + H - o) % H

    def send_maps(o):
        return remote(actm, mbuf.at[at(head * TR, TR)], m_send.at[o], m_recv.at[o], (c, peer(o)))

    def recv_maps(o):
        return remote(actm, mbuf.at[at(source(o) * TR, TR)], m_send.at[o], m_recv.at[o], (c, peer(o)))

    def send_x(k, o):
        return remote(
            act.at[k, peer(o)], xbuf.at[k, at(head * TR, TR)], x_send.at[k, o], x_recv.at[k, o], (c, peer(o))
        )

    def recv_x(k, o):
        return remote(
            act.at[k, peer(o)], xbuf.at[k, at(source(o) * TR, TR)], x_send.at[k, o], x_recv.at[k, o], (c, peer(o))
        )

    for i in range(2 * STATE // TILE):
        actm[:, i * TILE : (i + 1) * TILE] = convolve(inner + i * TILE)
    for o in order:
        send_maps(o).start()
    mbuf[at(head * TR, TR), :] = actm[...]

    def conv_chunk(k, carry):
        @pl.when(index > 0)
        def _():
            for p in range(H):
                send_halo(k * H + p, chunk_lanes(k, p)).wait_recv()

        for o in order + [0]:
            p = peer(o)
            for i in range(TPC):
                value = convolve(p * lanes + k * W + i * TILE)
                if o:
                    act[k, p, :, i * TILE : (i + 1) * TILE] = value
                else:
                    xbuf[k, at(head * TR, TR), i * TILE : (i + 1) * TILE] = value
            if o:
                send_x(k, o).start()
        return carry

    lax.fori_loop(0, K, conv_chunk, 0)

    def sums_chunk(k, carry):
        for b in range(NB):
            cums[k, b] = triangular(rate[at(k * GROUP, GROUP), b * BLOCK : (b + 1) * BLOCK], 0)
        return carry

    lax.fori_loop(0, K, sums_chunk, 0)

    for o in order:
        recv_maps(o).wait_recv()

    row = lax.broadcasted_iota(jnp.int32, (BLOCK, BLOCK), 0)
    col = lax.broadcasted_iota(jnp.int32, (BLOCK, BLOCK), 1)
    causal = row >= col
    for b in range(NB):
        m = mbuf[b * BLOCK : (b + 1) * BLOCK]
        aff[b] = jnp.where(causal, dot(m[:, STATE:], m[:, :STATE], 1, 1), 0.0)
        da[b] = jnp.zeros((BLOCK, BLOCK), F32)
    acc[...] = jnp.zeros_like(acc)

    stride = C // TPC

    def owner(k, j):
        return j * stride + (j + k) % stride

    def send_tile(q, k, j):
        return remote(
            tsend.at[q, k, j], inbox.at[q, k, c], t_send.at[q, k, j], t_recv.at[q, k, c], (owner(k, j), head)
        )

    def recv_tile(q, k, src):
        return remote(tsend.at[q, k, 0], inbox.at[q, k, src], t_send.at[q, k, 0], t_recv.at[q, k, src], (src, head))

    def pass_on(q, k, decay):
        high = decay.astype(BF16).astype(F32)
        both = jnp.concatenate([high, decay - high], axis=0).astype(BF16)
        for j in range(TPC):
            where = slice(j * TILE, (j + 1) * TILE)
            tsend[q, k, j, :STATE] = t_ref[:, where].astype(BF16)
            tsend[q, k, j, STATE:] = both[:, where]
        for j in range(TPC):
            @pl.when(owner(k, j) == c)
            def _():
                inbox[q, k, c] = tsend[q, k, j]

            @pl.when(owner(k, j) != c)
            def _():
                send_tile(q, k, j).start()

    def pulls(k, carry):
        t_ref[...] = jnp.zeros_like(t_ref)
        d_ref[k] = jnp.ones(d_ref.shape[1:], F32)

        def block(b, carry):
            rows = at(b * BLOCK, BLOCK)
            from_start = expand(jnp.exp(cums[k, b]), W, head_dim)
            dyw = (dy[rows, at(k * W, W)].astype(F32) * from_start).astype(BF16)
            grad = dot(mbuf[rows, STATE:], dyw, 0, 0)
            last_dec = from_start[BLOCK - 1 :]
            gp[k, b] = grad
            dec[k, b] = jnp.broadcast_to(last_dec, (GROUP, W))
            t_ref[...] = t_ref[...] + d_ref[k, 0:1] * grad
            d_ref[k] = d_ref[k] * last_dec
            return carry

        lax.fori_loop(0, NB, block, 0)
        pass_on(1, k, d_ref[k])
        return carry

    dy_copy.wait()
    lax.fori_loop(0, K, pulls, 0)

    def states(k):
        t_ref[...] = jnp.zeros_like(t_ref)

        def block(b, carry):
            rows = at(b * BLOCK, BLOCK)
            cum = cums[k, b]
            to_end = expand(jnp.exp(cum[:, BLOCK - 1 :] - cum) * step[at(k * GROUP, GROUP), rows], W, head_dim)
            xw = (xbuf[k, rows, :].astype(F32) * to_end).astype(BF16)
            more = dot(mbuf[rows, :STATE], xw, 0, 0)
            inc[k, b] = more
            t_ref[...] = t_ref[...] * dec[k, b, 0:1] + more
            return carry

        lax.fori_loop(0, NB, block, 0)
        pass_on(0, k, d_ref[k])

    def send_enter(q, k, j, dst):
        return remote(outbox.at[q, k, dst], ent.at[q, k, j], e_send.at[q, k, dst], e_recv.at[q, k, j], (dst, head))

    def chain(q, k):
        j = c // stride

        @pl.when(c == owner(k, j))
        def _():
            def arrive(src, carry):
                @pl.when(src != c)
                def _():
                    recv_tile(q, k, src).wait_recv()
                return carry

            lax.fori_loop(0, C, arrive, 0)

            def follow(i, state):
                i = C - 1 - i if q else i
                outbox[q, k, i] = state.astype(BF16)
                both = inbox[q, k, i, STATE:].astype(F32)
                return (both[0:1] + both[GROUP : GROUP + 1]) * state + inbox[q, k, i, :STATE].astype(F32)

            lax.fori_loop(0, C, follow, jnp.zeros((STATE, TILE), F32))

            def leave(dst, carry):
                @pl.when(dst != c)
                def _():
                    send_enter(q, k, j, dst).start()
                return carry

            lax.fori_loop(0, C, leave, 0)
            ent[q, k, j] = outbox[q, k, c]

    half = BLOCK // 2
    pair = 2 * head_dim

    def intra(k):
        first = lax.broadcasted_iota(jnp.int32, (half, pair), 1) < head_dim

        def each(value):
            none = jnp.zeros_like(value)
            return jnp.concatenate([jnp.where(first, value, none), jnp.where(first, none, value)], axis=0)

        def block(b, carry):
            rows = at(b * BLOCK, BLOCK)
            cum = cums[k, b]
            cum_col = cum.T
            dyb = dy[rows, at(k * W, W)]
            steps = expand(step[at(k * GROUP, GROUP), rows], W, head_dim)
            xsf = xbuf[k, rows, :].astype(F32) * steps
            xs = xsf.astype(BF16)
            middle = cum[:, half - 1 : half]
            until = expand(jnp.exp(middle - cum[:, :half]), W, head_dim)
            since = expand(jnp.exp(cum[:, half:] - middle), W, head_dim)
            early = (xsf[:half] * until).astype(BF16)
            late = (dyb[half:].astype(F32) * since).astype(BF16)
            across = aff[b, half:, :half].astype(BF16)
            ins_late = since * dot(across, early, 1, 0)
            back_early = until * dot(across, late, 0, 0)
            da[b, half:, :half] += dot(late, early, 1, 1)
            for part in range(2):
                side = slice(part * half, (part + 1) * half)
                near = aff[b, side, side]
                near_da = jnp.zeros((half, half), F32)
                for p in range(GROUP // 2):
                    where = slice(p * pair, (p + 1) * pair)
                    xs_p, dy_p = each(xs[side, where]), dyb[side, where]
                    decays = [
                        jnp.exp(jnp.minimum(cum_col[side, h : h + 1] - cum[h : h + 1, side], 0.0))
                        for h in (2 * p, 2 * p + 1)
                    ]
                    weights = [(near * decay).astype(BF16) for decay in decays]
                    ins = dot(jnp.concatenate(weights, axis=1), xs_p, 1, 0)
                    back = dot(jnp.concatenate(weights, axis=0), each(dy_p), 0, 0)
                    both = dot(dy_p, xs_p, 1, 1)
                    near_da = near_da + both[:, :half] * decays[0] + both[:, half:] * decays[1]
                    if part:
                        ins = ins + ins_late[:, where]
                    else:
                        back = back + back_early[:, where]
                    y[at(b * BLOCK + part * half, half), at(k * W + p * pair, pair)] = ins.astype(BF16)
                    dxbuf[k, at(b * BLOCK + part * half, half), where] = back.astype(BF16)
                da[b, side, side] += near_da
            return carry

        lax.fori_loop(0, NB, block, 0)

    def send_back(k, o):
        return remote(
            dxbuf.at[k, at(peer(o) * TR, TR)], rbuf.at[k, head], b_send.at[k, o], b_recv.at[k, o], (c, peer(o))
        )

    def recv_back(k, o):
        return remote(
            dxbuf.at[k, at(peer(o) * TR, TR)], rbuf.at[k, source(o)], b_send.at[k, o], b_recv.at[k, o], (c, peer(o))
        )

    def store_y(k):
        wide = at(k * W, W)
        return pltpu.make_async_copy(y.at[:, wide], y_hbm.at[:, wide], y_sem.at[k])

    def store_gin(i, where):
        return pltpu.make_async_copy(gin.at[:, where], gin_hbm.at[:, where], gin_sem.at[i])

    def carry_over(k):
        for j in range(TPC):
            @pl.when(owner(k, j) != c)
            def _():
                for q in range(2):
                    remote(
                        outbox.at[q, k, 0], ent.at[q, k, j], e_send.at[q, k, 0], e_recv.at[q, k, j], (owner(k, j), head)
                    ).wait_recv()

        state = jnp.concatenate([ent[0, k, j] for j in range(TPC)], axis=1).astype(F32)
        grad = jnp.concatenate([ent[1, k, j] for j in range(TPC)], axis=1).astype(F32)
        grads = [None] * NB
        for b in range(NB - 1, -1, -1):
            grads[b] = grad
            g_ref[b] = grad.astype(BF16)
            if b > 0:
                grad = dec[k, b, 0:1] * grad + gp[k, b]
        for b in range(NB):
            s_ref[b] = state.astype(BF16)
            state = dec[k, b, 0:1] * state + inc[k, b]
            both = jnp.sum(state * grads[b], axis=0, keepdims=True)
            dots[b] = head_sums(jnp.broadcast_to(both, (TILE, W)), head_dim)

        lane_head = lax.broadcasted_iota(jnp.int32, (1, W), 1) // head_dim
        gain = jnp.zeros((1, W), F32)
        for h in range(GROUP):
            gain = jnp.where(lane_head == h, skip[k * GROUP + h], gain)

        def block(turn, carry):
            b = jnp.where(head < H // 2, NB - 1 - turn, turn)
            rows = at(b * BLOCK, BLOCK)
            heads = at(k * GROUP, GROUP)
            wide = at(k * W, W)
            cum = cums[k, b]
            sizes = step[heads, rows]
            from_start = expand(jnp.exp(cum), W, head_dim)
            ending = expand(jnp.exp(cum[:, BLOCK - 1 :] - cum), W, head_dim)
            steps = expand(sizes, W, head_dim)
            x = xbuf[k, rows, :].astype(F32)
            dyf = dy[rows, wide].astype(F32)
            enter, leave = s_ref[b], g_ref[b]
            in_map, out_map = mbuf[rows, :STATE], mbuf[rows, STATE:]
            out = y[rows, wide].astype(F32) + from_start * dot(out_map, enter, 1, 0)
            back = dxbuf[k, rows, :].astype(F32) + ending * dot(in_map, leave, 1, 0)
            y[rows, wide] = (out + gain * x).astype(BF16)
            dxbuf[k, rows, :] = (steps * back + gain * dyf).astype(BF16)
            by_step = head_sums(x * back, head_dim)
            gs[heads, rows] = by_step
            gc = head_sums(dyf * out, head_dim) - sizes * by_step
            place = lax.broadcasted_iota(jnp.int32, gc.shape, 1)
            gc = gc + jnp.where(place == BLOCK - 1, dots[b][:, 0:1], 0.0)
            gd[heads, rows] = triangular(gc, 1)
            acc[rows, :STATE] += dot((x * steps * ending).astype(BF16), leave, 1, 1)
            acc[rows, STATE:] += dot((dyf * from_start).astype(BF16), enter, 1, 1)
            for o in order:
                low, high = peer(o) * TR // BLOCK, (peer(o) * TR + TR - 1) // BLOCK

                @pl.when(b == jnp.where(head < H // 2, low, high))
                def _():
                    send_back(k, o).start()
            return carry

        lax.fori_loop(0, NB, block, 0)
        store_y(k).start()
        rbuf[k, head] = dxbuf[k, at(head * TR, TR), :]

    def send_mapgrad(o):
        return remote(gms.at[at(peer(o) * TR, TR)], gmr.at[head], g_send.at[o], g_recv.at[o], (c, peer(o)))

    def recv_mapgrad(o):
        return remote(gms.at[at(peer(o) * TR, TR)], gmr.at[source(o)], g_send.at[o], g_recv.at[o], (c, peer(o)))

    def send_edge(k, wide):
        return remote(
            hsend.at[k, :, pl.ds(0, wide)], hrecv.at[k, :, pl.ds(0, wide)], h_send.at[k], h_recv.at[k], preceding
        )

    def edge(k, wide):
        @pl.when(index > 0)
        def _():
            send_edge(k, wide).start()

    def arrive_edge(k, wide):
        @pl.when(index < total - 1)
        def _():
            send_edge(k, wide).wait_recv()

        @pl.when(index == total - 1)
        def _():
            hrecv[k] = jnp.zeros(hrecv.shape[1:], F32)

    def unwind(grad_pre, tail, where):
        padded = jnp.concatenate([grad_pre, tail], axis=0)
        out = cw[taps - 1 : taps, where] * grad_pre
        for tap in range(taps - 2, -1, -1):
            begin = taps - 1 - tap
            out = out + cw[tap : tap + 1, where] * padded[begin : begin + TR]
        gin[:, where] = out.astype(BF16)

    def first_rows(k):
        for o in order:
            recv_back(k, o).wait_recv()
        for p in range(H):
            where = at(p * lanes + k * W, W)
            top = rbuf[k, p, :16].astype(F32) * dsil[:16, where].astype(F32)
            hsend[k, :, p * W : (p + 1) * W] = top[:8]
        edge(k, H * W)

    def last_rows(k):
        arrive_edge(k, H * W)
        for p in range(H):
            for i in range(TPC):
                where = at(p * lanes + k * W + i * TILE, TILE)
                inside = slice(i * TILE, (i + 1) * TILE)
                grad_pre = rbuf[k, p, :, inside].astype(F32) * dsil[:, where].astype(F32)
                unwind(grad_pre, hrecv[k, :, p * W + i * TILE : p * W + (i + 1) * TILE], where)
            store_gin(k * H + p, chunk_lanes(k, p)).start()

    def stage(k, carry):
        @pl.when(k < K)
        def _():
            for o in order:
                recv_x(k, o).wait_recv()
            states(k)
            chain(1, k)

        @pl.when(k < K - 1)
        def _():
            intra(k)
            chain(0, k)

        @pl.when(k >= 1)
        def _():
            carry_over(k - 1)

        @pl.when(k == K - 1)
        def _():
            chain(0, k)
            intra(k)

        @pl.when(k >= 2)
        def _():
            first_rows(k - 2)

        @pl.when(k >= 3)
        def _():
            last_rows(k - 3)

        return carry

    lax.fori_loop(0, K + 1, stage, 0)

    for b in range(NB):
        rows = slice(b * BLOCK, (b + 1) * BLOCK)
        grad = jnp.where(causal, da[b], 0.0).astype(BF16)
        gms[rows, :STATE] = (acc[rows, :STATE] + dot(grad, mbuf[rows, STATE:], 0, 0)).astype(BF16)
        gms[rows, STATE:] = (acc[rows, STATE:] + dot(grad, mbuf[rows, :STATE], 1, 0)).astype(BF16)
    for o in order:
        send_mapgrad(o).start()
    gmr[head] = gms[at(head * TR, TR), :]

    for k in range(max(K - 2, 0), K - 1):
        last_rows(k)
    first_rows(K - 1)
    for o in order:
        recv_mapgrad(o).wait_recv()
    parts = []
    for i in range(2 * STATE // TILE):
        inside = slice(i * TILE, (i + 1) * TILE)
        summed = gmr[0, :, inside].astype(F32)
        for p in range(1, H):
            summed = summed + gmr[p, :, inside].astype(F32)
        grad_pre = summed.astype(BF16).astype(F32) * dsil[:, inner + i * TILE : inner + (i + 1) * TILE].astype(F32)
        parts.append(grad_pre)
        hsend[K, :, inside] = grad_pre[:8]
    edge(K, 2 * STATE)
    last_rows(K - 1)
    arrive_edge(K, 2 * STATE)
    for i in range(2 * STATE // TILE):
        inside = slice(i * TILE, (i + 1) * TILE)
        unwind(parts[i], hrecv[K, :, inside], slice(inner + i * TILE, inner + (i + 1) * TILE))

    store_gin(K * H, map_lanes).start()

    @pl.when(index < total - 1)
    def _():
        send_halo(K * H, map_lanes).wait_send()

        def drain_halo(i, carry):
            send_halo(i, chunk_lanes(i // H, i % H)).wait_send()
            return carry

        lax.fori_loop(0, K * H, drain_halo, 0)

    for o in order:
        send_maps(o).wait_send()
        send_mapgrad(o).wait_send()

    def drain(k, carry):
        for o in order:
            send_x(k, o).wait_send()
            send_back(k, o).wait_send()
        for q in range(2):
            for j in range(TPC):
                @pl.when(owner(k, j) != c)
                def _():
                    send_tile(q, k, j).wait_send()

        @pl.when(c == owner(k, c // stride))
        def _():
            def leave(dst, carry):
                @pl.when(dst != c)
                def _():
                    for q in range(2):
                        send_enter(q, k, c // stride, dst).wait_send()
                return carry

            lax.fori_loop(0, C, leave, 0)

        return carry

    lax.fori_loop(0, K, drain, 0)

    def stored(k, carry):
        store_y(k).wait()
        for p in range(H):
            store_gin(k * H + p, chunk_lanes(k, p)).wait()
        return carry

    lax.fori_loop(0, K, stored, 0)
    store_gin(K * H, map_lanes).wait()

    @pl.when(index > 0)
    def _():
        def drain_edges(k, carry):
            send_edge(k, H * W).wait_send()
            return carry

        lax.fori_loop(0, K, drain_edges, 0)
        send_edge(K, 2 * STATE).wait_send()


def hand_on_kernel(count, *refs):
    ins, outs, held = refs[:count], refs[count : 2 * count], refs[2 * count : 3 * count]
    in_sem, out_sem = refs[3 * count :]
    loads, stores = [], []
    for source, target, keep in zip(ins, outs, held):
        rows = source.shape[0]
        pieces = 6 if rows % 96 == 0 else 1
        for i in range(pieces):
            part = pl.ds(i * (rows // pieces), rows // pieces)
            loads.append(pltpu.make_async_copy(source.at[part], keep.at[part], in_sem.at[len(loads)]))
            stores.append(pltpu.make_async_copy(keep.at[part], target.at[part], out_sem.at[len(stores)]))
    for load in loads:
        load.start()
    for load, store in zip(loads, stores):
        load.wait()
        store.start()
    for store in stores:
        store.wait()


def hand_on(arrays):
    anywhere = pl.BlockSpec(memory_space=pl.ANY)
    count = len(arrays)
    return pl.pallas_call(
        partial(hand_on_kernel, count),
        out_shape=[jax.ShapeDtypeStruct(a.shape, a.dtype) for a in arrays],
        in_specs=[anywhere] * count,
        out_specs=[anywhere] * count,
        scratch_shapes=[pltpu.VMEM(a.shape, a.dtype) for a in arrays]
        + [pltpu.SemaphoreType.DMA((6 * count,))] * 2,
        compiler_params=pltpu.CompilerParams(vmem_limit_bytes=VMEM_LIMIT),
        name="hand_on",
    )(*arrays)


def local(conv_input, conv_weight, conv_bias, step_size, log_decay, skip_gain, grad_output):
    tok_rows, channels = conv_input.shape
    heads_here, seq_rows = step_size.shape
    lanes = grad_output.shape[1]
    head_dim = lanes // heads_here
    H = lax.axis_size("head")
    C = lax.axis_size("ctx")
    K = heads_here // GROUP
    W = GROUP * head_dim
    NB = seq_rows // BLOCK
    TPC = W // TILE
    packed = STATE + 2 * GROUP
    dma = pltpu.SemaphoreType.DMA
    vmem = pl.BlockSpec(memory_space=pltpu.VMEM)
    results = pl.pallas_call(
        partial(mixer_kernel, H, C, head_dim),
        out_shape=[
            jax.ShapeDtypeStruct((seq_rows, lanes), BF16),
            jax.ShapeDtypeStruct((tok_rows, channels), BF16),
            jax.ShapeDtypeStruct((heads_here, seq_rows), F32),
            jax.ShapeDtypeStruct((heads_here, seq_rows), F32),
        ],
        in_specs=[vmem] * 5 + [pl.BlockSpec(memory_space=pltpu.SMEM), pl.BlockSpec(memory_space=pl.ANY)],
        out_specs=[pl.BlockSpec(memory_space=pl.ANY)] * 2 + [vmem] * 2,
        scratch_shapes=[
            pltpu.VMEM((seq_rows, lanes), BF16),
            pltpu.VMEM((seq_rows, lanes), BF16),
            pltpu.VMEM((tok_rows, channels), BF16),
            pltpu.VMEM((16, channels), BF16),
            pltpu.VMEM((K, H, tok_rows, W), BF16),
            pltpu.VMEM((tok_rows, 2 * STATE), BF16),
            pltpu.VMEM((tok_rows, channels), BF16),
            pltpu.VMEM((K, seq_rows, W), BF16),
            pltpu.VMEM((seq_rows, 2 * STATE), BF16),
            pltpu.VMEM((K, NB, GROUP, BLOCK), F32),
            pltpu.VMEM((NB, BLOCK, BLOCK), F32),
            pltpu.VMEM((NB, BLOCK, BLOCK), F32),
            pltpu.VMEM((K, NB, STATE, W), F32),
            pltpu.VMEM((K, NB, STATE, W), F32),
            pltpu.VMEM((K, NB, GROUP, W), F32),
            pltpu.VMEM((STATE, W), F32),
            pltpu.VMEM((K, GROUP, W), F32),
            pltpu.VMEM((2, K, TPC, packed, TILE), BF16),
            pltpu.VMEM((2, K, C, packed, TILE), BF16),
            pltpu.VMEM((2, K, C, STATE, TILE), BF16),
            pltpu.VMEM((2, K, TPC, STATE, TILE), BF16),
            pltpu.VMEM((NB, STATE, W), BF16),
            pltpu.VMEM((NB, STATE, W), BF16),
            pltpu.VMEM((NB, GROUP, TILE), F32),
            pltpu.VMEM((K, seq_rows, W), BF16),
            pltpu.VMEM((K, H, tok_rows, W), BF16),
            pltpu.VMEM((seq_rows, 2 * STATE), F32),
            pltpu.VMEM((seq_rows, 2 * STATE), BF16),
            pltpu.VMEM((H, tok_rows, 2 * STATE), BF16),
            pltpu.VMEM((K + 1, 8, H * W), F32),
            pltpu.VMEM((K + 1, 8, H * W), F32),
            dma,
            dma((K,)),
            dma((K * H + 1,)),
            dma((K * H + 1,)),
            dma((K * H + 1,)),
            dma((K, H)),
            dma((K, H)),
            dma((H,)),
            dma((H,)),
            dma((2, K, TPC)),
            dma((2, K, C)),
            dma((2, K, C)),
            dma((2, K, TPC)),
            dma((K, H)),
            dma((K, H)),
            dma((H,)),
            dma((H,)),
            dma((K + 1,)),
            dma((K + 1,)),
        ],
        compiler_params=pltpu.CompilerParams(
            vmem_limit_bytes=VMEM_LIMIT, collective_id=0, has_side_effects=True
        ),
        cost_estimate=pl.CostEstimate(
            flops=30_000_000_000, bytes_accessed=13_000_000, transcendentals=10_000_000
        ),
        name="mixer",
    )(conv_input, conv_weight, conv_bias.reshape(-1, TILE), step_size, log_decay, skip_gain, grad_output)
    return tuple(hand_on(results))


def solution(mesh):
    return jax.shard_map(
        local,
        mesh=mesh,
        in_specs=(
            P(("ctx", "head"), None),
            P(),
            P(),
            P("head", "ctx"),
            P("head", "ctx"),
            P("head"),
            P("ctx", "head"),
        ),
        out_specs=(P("ctx", "head"), P(("ctx", "head"), None), P("head", "ctx"), P("head", "ctx")),
        check_vma=False,
    )
```
